512 devices in a mesh: dp: 8 (over y_hi, core), view: 8 (over z), tm: 8 (over x, y_lo).
Axes of the slice: x: 4, y: 8 (y_hi: 4, y_lo: 2; y = y_hi * 2 + y_lo), z: 8, core: 2. Of those that a mesh axis runs over, the one named last changes fastest.
Arguments:
- tokens: bfloat16 [8, 8, 1024, 1024], P('dp', 'view', 'tm'), may hold values from -24 to 24
- cotangent: bfloat16 [8, 8, 1024, 1024], P('dp', 'view', 'tm'), may hold values from -6 to 6
- w_query: bfloat16 [1024, 512], P(None, 'tm'), may hold values from -0.1875 to 0.1875
- w_key: bfloat16 [1024, 512], P(None, 'tm'), may hold values from -0.1875 to 0.1875
- w_value: bfloat16 [1024, 512], P(None, 'tm'), may hold values from -0.1875 to 0.1875
- w_out: bfloat16 [512, 1024], P('tm'), may hold values from -0.25 to 0.25
- masks: int32 [4, 8, 8], replicated, may hold values from 0 to 1, as said below
- rig_ids: int32 [8], P('dp'), may hold values from 0 to 3
Outputs:
- attended: bfloat16 [8, 8, 1024, 1024], P('dp', 'view', 'tm')
- grad_tokens: bfloat16 [8, 8, 1024, 1024], P('dp', 'view', 'tm')
- grad_query: float32 [1024, 512], P(None, 'tm')
- grad_key: float32 [1024, 512], P(None, 'tm')
- grad_value: float32 [1024, 512], P(None, 'tm')
- grad_out: float32 [512, 1024], P('tm')
The draws below stay inside these ranges and needn't reach their ends.
Inputs may be any that keep to these rules, and one draw needn't show every extreme that they name: `masks`: tile i of a time span is the 128 tokens of camera i // 1 that start at position (i % 1) * 128 of the span (with one tile a camera, tile i is the whole span of camera i); every query tile of every rig lists 1 to 4 key tiles, and every rig has a query tile that lists exactly 4.
All inputs are finite; a program needn't handle non-finite values.
Results may differ from the reference program's by a relative error of at most 0.02.
The reference program's roundings to bfloat16 on the way count: a program that leaves them out, or rounds other values in their place, can miss the bound.
Values may be sent and summed in bfloat16 or wider, within the bound.
A program may use at most 64 MiB of HBM per device.

```python
import math
import jax
import jax.numpy as jnp
from jax import lax

D = 1024
HEADS = 8
HEAD_DIM = 64
TILE = 128
NRIG = 4
TQ = 128
HE = 512
VT = 8
MOST = 4
CLIPS = 8
CAMS = 8
SEQ = 1024


def draw_tokens(key, part):
    key = jax.random.fold_in(key, 9)
    first_key = jax.random.fold_in(key, 0)
    base = jax.random.normal(first_key, (CLIPS, CAMS, SEQ, D), jnp.float32)
    values = jnp.clip(base, -6.0, 6.0)
    return values.astype(jnp.bfloat16)


def draw_cotangent(key, part):
    key = jax.random.fold_in(key, 13)
    base = jnp.clip(jax.random.normal(key, (CLIPS, CAMS, SEQ, D), jnp.float32), -6.0, 6.0)
    clip_index = jnp.arange(CLIPS, dtype=jnp.float32)[:, None]
    cam_index = jnp.arange(CAMS, dtype=jnp.float32)[None, :]
    position = (clip_index * CAMS + cam_index) / (CLIPS * CAMS - 1)
    block_scale = jnp.exp((position - 1.0) * math.log(32.0))
    return (base * block_scale[:, :, None, None]).astype(jnp.bfloat16)


def draw_masks(key, part):
    key = jax.random.fold_in(key, 5)
    count_key, order_key = jax.random.split(key)
    listed = jax.random.randint(count_key, (NRIG, VT), 1, MOST + 1)
    rig_index = jnp.arange(NRIG, dtype=jnp.int32)[:, None]
    row_index = jnp.arange(VT, dtype=jnp.int32)[None, :]
    listed = jnp.minimum(listed + rig_index, MOST)
    listed = jnp.where(row_index == rig_index * 3 % VT, MOST, listed)
    ranking = jax.random.randint(order_key, (NRIG, VT, VT), 0, 1 << 20) * VT + jnp.arange(VT, dtype=jnp.int32)
    placing = jnp.argsort(jnp.argsort(ranking, axis=-1), axis=-1)
    return (placing < listed[:, :, None]).astype(jnp.int32)


def plant(drawn, own_key, low, high):
    place = [jax.random.randint(jax.random.fold_in(own_key, axis), (), 0, length) for axis, length in enumerate(drawn.shape)]
    widest = drawn.shape.index(max(drawn.shape))
    beside = place[:widest] + [(place[widest] + 1) % drawn.shape[widest]] + place[widest + 1:]
    return drawn.at[tuple(place)].set(low).at[tuple(beside)].set(high)


def block_levels(own_key, dims, shards, low, top_value):
    def one(axis_at, parts):
        draws = jax.random.uniform(jax.random.fold_in(jax.random.fold_in(own_key, 6), axis_at), (parts,), jnp.float32, low / len(shards), top_value / len(shards))
        return jnp.repeat(jnp.exp(draws), dims[axis_at] // parts).reshape((-1,) + (1,) * (len(dims) - axis_at - 1))

    gain = one(*shards[0])
    for cut in shards[1:]:
        gain = gain * one(*cut)
    return gain


def noise(rng, extent, scale, most, shards=(), kind=jnp.bfloat16):
    factor_of = block_levels(rng, extent, shards, -0.22, 0.18) if shards else 1.0
    values = jax.random.normal(rng, extent, jnp.float32) * scale * factor_of
    return jnp.minimum(jnp.maximum(values, -most), most).astype(kind)


def setup_inputs(seed: int = 0) -> dict:
    keys = jax.random.split(jax.random.key(seed), 9)
    tokens = draw_tokens(jax.random.fold_in(keys[8], 71), 0)
    cotangent = draw_cotangent(jax.random.fold_in(keys[8], 71), 0)
    w_query = noise(keys[2], (D, HE), D ** -0.5, 0.1875, ((1, 8),))
    w_key = noise(keys[3], (D, HE), D ** -0.5, 0.1875, ((1, 8),))
    w_value = noise(keys[4], (D, HE), D ** -0.5, 0.1875, ((1, 8),))
    w_out = noise(keys[5], (HE, D), HE ** -0.5, 0.25, ((0, 8),))
    masks = draw_masks(jax.random.fold_in(keys[8], 71), 0)
    rig_ids = plant(jax.random.randint(keys[7], (CLIPS,), 0, NRIG), jax.random.fold_in(keys[7], 1), 0, NRIG - 1).astype(jnp.int32)
    return {"tokens": tokens, "cotangent": cotangent, "w_query": w_query, "w_key": w_key, "w_value": w_value, "w_out": w_out, "masks": masks, "rig_ids": rig_ids}


def expand_tiles(tile_grid, tile_size):
    grid_rows, grid_cols = tile_grid.shape
    spread = jnp.broadcast_to(tile_grid[:, None, :, None], (grid_rows, tile_size, grid_cols, tile_size))
    return spread.reshape(grid_rows * tile_size, grid_cols * tile_size) == 1


def block_pass(tok_rows, cot_rows, allowed, w_query, w_key, w_value, w_out, cameras):
    count = tok_rows.shape[0]
    factor = HEAD_DIM ** -0.5
    query_rows = jnp.dot(tok_rows, w_query, preferred_element_type=jnp.float32).astype(jnp.bfloat16)
    key_rows = jnp.dot(tok_rows, w_key, preferred_element_type=jnp.float32).astype(jnp.bfloat16)
    value_rows = jnp.dot(tok_rows, w_value, preferred_element_type=jnp.float32).astype(jnp.bfloat16)
    query_heads = query_rows.astype(jnp.float32).reshape(count, HEADS, HEAD_DIM)
    key_heads = key_rows.astype(jnp.float32).reshape(count, HEADS, HEAD_DIM)
    value_heads = value_rows.astype(jnp.float32).reshape(count, HEADS, HEAD_DIM)
    scores = jnp.einsum("qhe,khe->hqk", query_heads, key_heads) * factor
    scores = jnp.where(allowed[None], scores, -1e30)
    highest = jnp.max(scores, axis=-1, keepdims=True)
    weights = jnp.where(allowed[None], jnp.exp(scores - highest), 0.0)
    probs_full = weights / jnp.sum(weights, axis=-1, keepdims=True)
    probs_half = probs_full.astype(jnp.bfloat16)
    attn_rows = jnp.einsum("hqk,khe->qhe", probs_half.astype(jnp.float32), value_heads)
    attn_rows = attn_rows.reshape(count, HEADS * HEAD_DIM).astype(jnp.bfloat16)
    attended = jnp.dot(attn_rows, w_out, preferred_element_type=jnp.float32).astype(jnp.bfloat16)
    grad_attn = jnp.dot(cot_rows, w_out.T, preferred_element_type=jnp.float32).astype(jnp.bfloat16)
    grad_heads = grad_attn.astype(jnp.float32).reshape(count, HEADS, HEAD_DIM)
    grad_probs = jnp.einsum("qhe,khe->hqk", grad_heads, value_heads)
    row_terms = jnp.sum(grad_heads * attn_rows.astype(jnp.float32).reshape(count, HEADS, HEAD_DIM), axis=-1).T
    grad_scores = (probs_full * (grad_probs - row_terms[:, :, None]) * factor).astype(jnp.bfloat16)
    grad_query = jnp.einsum("hqk,khe->qhe", grad_scores.astype(jnp.float32), key_heads)
    grad_query = grad_query.reshape(count, HEADS * HEAD_DIM).astype(jnp.bfloat16)
    per_camera = count // cameras
    scores_cam = grad_scores.astype(jnp.float32).reshape(HEADS, cameras, per_camera, count)
    query_cam = query_heads.reshape(cameras, per_camera, HEADS, HEAD_DIM)
    key_parts = jnp.einsum("hapk,aphe->akhe", scores_cam, query_cam).astype(jnp.bfloat16)
    key_parts = lax.optimization_barrier(key_parts)
    grad_key = jnp.sum(key_parts.astype(jnp.float32), axis=0).reshape(count, HEADS * HEAD_DIM).astype(jnp.bfloat16)
    probs_cam = probs_half.astype(jnp.float32).reshape(HEADS, cameras, per_camera, count)
    grad_cam = grad_heads.reshape(cameras, per_camera, HEADS, HEAD_DIM)
    value_parts = jnp.einsum("hapk,aphe->akhe", probs_cam, grad_cam).astype(jnp.bfloat16)
    value_parts = lax.optimization_barrier(value_parts)
    grad_value = jnp.sum(value_parts.astype(jnp.float32), axis=0).reshape(count, HEADS * HEAD_DIM).astype(jnp.bfloat16)
    grad_rows = (jnp.dot(grad_query, w_query.T, preferred_element_type=jnp.float32)
                 + jnp.dot(grad_key, w_key.T, preferred_element_type=jnp.float32)
                 + jnp.dot(grad_value, w_value.T, preferred_element_type=jnp.float32)).astype(jnp.bfloat16)
    weight_terms = (jnp.dot(tok_rows.T, grad_query, preferred_element_type=jnp.float32),
                    jnp.dot(tok_rows.T, grad_key, preferred_element_type=jnp.float32),
                    jnp.dot(tok_rows.T, grad_value, preferred_element_type=jnp.float32),
                    jnp.dot(attn_rows.T, cot_rows, preferred_element_type=jnp.float32))
    return attended, grad_rows, weight_terms


def reference(tokens, cotangent, w_query, w_key, w_value, w_out, masks, rig_ids):
    clip_count, cameras, positions, width = tokens.shape
    span_count = positions // TQ
    inner = HEADS * HEAD_DIM

    def one_block(carry, block_id):
        clip_id = block_id // span_count
        span_id = block_id % span_count
        anchor = (clip_id, jnp.int32(0), span_id * TQ, jnp.int32(0))
        tok_rows = lax.dynamic_slice(tokens, anchor, (1, cameras, TQ, width)).reshape(cameras * TQ, width)
        cot_rows = lax.dynamic_slice(cotangent, anchor, (1, cameras, TQ, width)).reshape(cameras * TQ, width)
        rig_table = lax.dynamic_index_in_dim(masks, rig_ids[clip_id], 0, keepdims=False)
        allowed = expand_tiles(rig_table, TILE)
        attended, grad_rows, weight_terms = block_pass(tok_rows, cot_rows, allowed, w_query, w_key, w_value, w_out, cameras)
        carry = tuple(total + term for total, term in zip(carry, weight_terms))
        return carry, (attended, grad_rows)

    start_sums = (jnp.zeros((width, inner), jnp.float32), jnp.zeros((width, inner), jnp.float32),
                  jnp.zeros((width, inner), jnp.float32), jnp.zeros((inner, width), jnp.float32))
    block_ids = jnp.arange(clip_count * span_count, dtype=jnp.int32)
    sums, (attended, grad_rows) = lax.scan(one_block, start_sums, block_ids)

    def arrange(stacked):
        stacked = stacked.reshape(clip_count, span_count, cameras, TQ, width)
        return jnp.transpose(stacked, (0, 2, 1, 3, 4)).reshape(clip_count, cameras, positions, width)

    return arrange(attended), arrange(grad_rows), sums[0], sums[1], sums[2], sums[3]
```

```python
import functools

import jax
import jax.numpy as jnp
from jax import lax
from jax.experimental import pallas as pl
from jax.experimental.pallas import tpu as pltpu
from jax.sharding import PartitionSpec as P

MESH = pl.DeviceIdType.MESH
BF16 = jnp.bfloat16
F32 = jnp.float32

KW, KS, KT, KC, KP, KX1, KX2, KB1, KB2, KR, KZ, KY, KF, KG = range(14)
KINDS = 14

NT = (((1,), (1,)), ((), ()))


def dot(a, b):
    return jnp.dot(a, b, preferred_element_type=F32)


def dot_nt(a, b):
    return lax.dot_general(a, b, NT, preferred_element_type=F32)


def kernel(
    n_d, n_z, n_t, depth,
    tok_ref, cot_ref, w_ref, masks_ref, rig_ref,
    att_ref, gtok_ref, g_ref,
    w_all, tok_all, cot_all, p_send, p_all, kv_t, acc, x1, x2, xa1, xa2, xb1, xb2,
    g_sum, c_send, c_recv, z_send, z_recv, y_recv, fin,
    ssem, rsem,
):
    rows, width = tok_ref.shape
    lanes = 2 * depth
    n_x = n_t // 2
    n_y = n_d // 2
    dp, z, tm = lax.axis_index("dp"), lax.axis_index("view"), lax.axis_index("tm")
    core, yh = dp % 2, dp // 2
    x, yl = tm // 2, tm % 2
    sib = dp + 1 - 2 * core

    def copy(src, dst, kind, at, **to):
        return pltpu.make_async_remote_copy(
            src_ref=src, dst_ref=dst, send_sem=ssem.at[kind, at], recv_sem=rsem.at[kind, at],
            device_id=to, device_id_type=MESH,
        )

    barrier = pltpu.get_barrier_semaphore()
    greeted = 0
    for s in range(1, n_t):
        pl.semaphore_signal(barrier, inc=1, device_id={"tm": (tm + s) % n_t}, device_id_type=MESH)
        greeted += 1
    for s in range(1, n_z):
        pl.semaphore_signal(barrier, inc=1, device_id={"view": (z + s) % n_z}, device_id_type=MESH)
        greeted += 1
    for s in range(1, n_y):
        pl.semaphore_signal(barrier, inc=1, device_id={"dp": (dp + 2 * s) % n_d}, device_id_type=MESH)
        greeted += 1
    pl.semaphore_signal(barrier, inc=1, device_id={"dp": sib}, device_id_type=MESH)
    greeted += 1
    pl.semaphore_wait(barrier, greeted)

    def offsets(step):
        g = step // 2
        dx = g + g // 2 - 2 * (g // 3) if n_x == 4 else g
        return dx, step % 2

    def peer(step):
        dx, dy = offsets(step)
        return ((x + dx) % n_x) * 2 + (yl + dy) % 2

    def source(step):
        dx, dy = offsets(step)
        return ((x - dx + n_x) % n_x) * 2 + (yl + dy) % 2

    half = width // 2
    mine = pl.ds(pl.multiple_of(core * half, half), half)
    for step in range(1, n_t):
        copy(w_ref.at[mine], w_all.at[tm, mine], KW, step, tm=peer(step)).start()
    w_all[tm] = w_ref[...]
    tok_all[tm] = tok_ref[...]
    cot_all[tm] = cot_ref[...]

    first = lax.broadcasted_iota(jnp.int32, (rows, lanes), 1) < depth

    def project(head):
        weights = w_all[head]
        by_tok = dot(tok_ref[...], weights)
        by_cot = dot(cot_ref[...], weights[:, :lanes])
        p_send[head, :, :lanes] = jnp.where(first, by_tok[:, :lanes], by_cot).astype(BF16)
        p_send[head, :, lanes:] = by_tok[:, lanes:].astype(BF16)

        @pl.when(head == z)
        def _():
            p_all[z] = p_send[head]

        @pl.when(head != z)
        def _():
            copy(p_send.at[head], p_all.at[z], KP, (head - z + n_z) % n_z, view=head).start()

    def w_part(step):
        return w_all.at[source(step), mine]

    def w_step(step, _):
        copy(w_part(step), w_part(step), KW, step, tm=peer(step)).wait_recv()
        copy(w_part(step), w_part(step), KS, step, dp=sib).start()

        @pl.when(step > 1)
        def _():
            w_other(step - 1)

        project(source(step - 1))
        return 0

    theirs = pl.ds(pl.multiple_of((1 - core) * half, half), half)

    def w_other(step):
        part = w_all.at[source(step), theirs]
        copy(part, part, KS, step, dp=sib).wait_recv()

    lax.fori_loop(1, n_t, w_step, 0)
    w_other(n_t - 1)
    project(source(n_t - 1))

    for step in range(1, n_t):
        copy(tok_ref, tok_all.at[tm], KT, step, tm=peer(step)).start()
        copy(cot_ref, cot_all.at[tm], KC, step, tm=peer(step)).start()

    for d in range(1, n_z):
        copy(p_send.at[0], p_all.at[(z - d + n_z) % n_z], KP, d, view=(z + d) % n_z).wait_recv()

    total = n_z * rows
    kv_t[...] = p_all[:, :, lanes:].reshape(total, lanes).T
    acc[...] = jnp.zeros_like(acc)
    rig = rig_ref[0]
    factor = depth ** -0.5

    def attend(cam, _):
        qd = p_all[cam, :, :lanes]
        zero = jnp.zeros_like(qd)
        block = jnp.concatenate([jnp.where(first, qd, zero), jnp.where(first, zero, qd)], axis=0)
        kv = p_all[:, :, lanes:].reshape(total, lanes)
        both = dot_nt(kv, block)
        scores = jnp.concatenate(
            [
                both[b * rows:(b + 1) * rows, :rows] * factor
                + (masks_ref[rig, cam, b] - 1).astype(F32) * 1e30
                for b in range(n_z)
            ],
            axis=0,
        )
        weights = jnp.exp(scores - jnp.max(scores, axis=0, keepdims=True))
        probs = weights * (1.0 / jnp.sum(weights, axis=0, keepdims=True))
        probs_half = probs.astype(BF16)
        attn = dot(kv_t[depth:], probs_half)
        grad_attn = qd.astype(F32).T[depth:]
        delta = jnp.sum(grad_attn * attn.astype(BF16).astype(F32), axis=0, keepdims=True)
        dscore = (probs * (both[:, rows:] - delta) * factor).astype(BF16)
        dq = dot(kv_t[:depth], dscore)
        x1[cam] = jnp.concatenate([dq, attn], axis=0).T.astype(BF16)

        @pl.when(cam == z)
        def _():
            xa1[z] = x1[cam]

        @pl.when(cam != z)
        def _():
            copy(x1.at[cam], xa1.at[z], KX1, (cam - z + n_z) % n_z, view=cam).start()

        part = dot(jnp.concatenate([dscore, probs_half], axis=1), block)
        acc[...] += part.astype(BF16).astype(F32)
        return 0

    lax.fori_loop(0, n_z, attend, 0)
    x2[...] = acc[...].astype(BF16).reshape(n_z, rows, lanes)
    for d in range(1, n_z):
        cam = (z + d) % n_z
        copy(x2.at[cam], xa2.at[z], KX2, d, view=cam).start()
    xa2[z] = x2[z]

    def hand_on(src, dst, kind, head):
        @pl.when(head == tm)
        def _():
            dst[tm] = src[head]

        @pl.when(head != tm)
        def _():
            copy(src.at[head], dst.at[tm], kind, (head - tm + n_t) % n_t, tm=head).start()

    def arrive1(d, _):
        head = (z - d + n_z) % n_z

        @pl.when(d > 0)
        def _():
            copy(xa1.at[head], xa1.at[head], KX1, d, view=head).wait_recv()

        hand_on(xa1, xb1, KB1, head)
        return 0

    def arrive2(d, _):
        head = (z - d + n_z) % n_z

        @pl.when(d > 0)
        def _():
            copy(xa2.at[head], xa2.at[head], KX2, d, view=head).wait_recv()

        hand_on(xa2, xb2, KB2, head)
        return 0

    lax.fori_loop(0, n_z, arrive1, 0)
    lax.fori_loop(0, n_z, arrive2, 0)

    for f in range(1, n_t):
        span = (tm - f + n_t) % n_t
        copy(xb1.at[span], xb1.at[span], KB1, f, tm=span).wait_recv()
        copy(xb2.at[span], xb2.at[span], KB2, f, tm=span).wait_recv()
    for step in range(1, n_t):
        span = source(step)
        copy(tok_all.at[span], tok_all.at[span], KT, step, tm=peer(step)).wait_recv()
        copy(cot_all.at[span], cot_all.at[span], KC, step, tm=peer(step)).wait_recv()

    b1 = xb1[...].reshape(n_t * rows, lanes).T
    b2 = xb2[...].reshape(n_t * rows, lanes).T
    tokens = tok_all[...].reshape(n_t * rows, width)
    cots = cot_all[...].reshape(n_t * rows, width)
    g_sum[:depth] = dot(b1[:depth], tokens)
    g_sum[depth:lanes] = dot(b1[depth:], cots)
    g_sum[lanes:] = dot(b2, tokens)

    keep = pl.ds(pl.multiple_of(core * lanes, lanes), lanes)
    give = pl.ds(pl.multiple_of((1 - core) * lanes, lanes), lanes)
    c_send[...] = g_sum[give].astype(BF16)
    core_copy = copy(c_send, c_recv, KR, 0, dp=sib)
    core_copy.start()
    core_copy.wait_recv()
    g_sum[keep] = g_sum[keep] + c_recv[...].astype(F32)
    z_send[...] = g_sum[keep].astype(BF16)

    chunk = lanes // n_z

    def rows_of(index):
        return pl.ds(pl.multiple_of(index * chunk, chunk), chunk)

    for d in range(1, n_z):
        cam = (z + d) % n_z
        copy(z_send.at[rows_of(cam)], z_recv.at[z], KZ, d, view=cam).start()

    def finish(head, sums):
        one, two = xa1[head], xa2[head]
        zero = jnp.zeros_like(one)
        left = jnp.concatenate(
            [
                jnp.concatenate([jnp.where(first, one, zero), two], axis=1),
                jnp.concatenate([jnp.where(first, zero, one), zero], axis=1),
            ],
            axis=0,
        )
        return sums + dot_nt(left, w_all[head])

    sums = lax.fori_loop(0, n_z, finish, jnp.zeros((2 * rows, width), F32))
    gtok_ref[...] = sums[:rows].astype(BF16)
    att_ref[...] = sums[rows:].astype(BF16)

    chunk_sum = z_send[rows_of(z)].astype(F32)
    for d in range(1, n_z):
        cam = (z - d + n_z) % n_z
        copy(z_recv.at[cam], z_recv.at[cam], KZ, d, view=cam).wait_recv()
        chunk_sum = chunk_sum + z_recv[cam].astype(F32)
    y_recv[yh] = chunk_sum.astype(BF16)

    for s in range(1, n_y):
        copy(y_recv.at[yh], y_recv.at[yh], KY, s, dp=(dp + 2 * s) % n_d).start()
    for s in range(1, n_y):
        other = (yh - s + n_y) % n_y
        copy(y_recv.at[other], y_recv.at[other], KY, s, dp=(dp + 2 * s) % n_d).wait_recv()
    all_sum = y_recv[0].astype(F32)
    for s in range(1, n_y):
        all_sum = all_sum + y_recv[s].astype(F32)

    def final_rows(side, index):
        return fin.at[pl.ds(pl.multiple_of(side * lanes + index * chunk, chunk), chunk)]

    fin[pl.ds(pl.multiple_of(core * lanes + z * chunk, chunk), chunk)] = all_sum.astype(BF16)
    for d in range(1, n_z):
        copy(final_rows(core, z), final_rows(core, z), KF, d, view=(z + d) % n_z).start()
    copy(final_rows(core, z), final_rows(core, z), KG, 0, dp=sib).start()
    for d in range(1, n_z):
        cam = (z - d + n_z) % n_z
        copy(final_rows(core, cam), final_rows(core, cam), KF, d, view=cam).wait_recv()
        copy(final_rows(core, cam), final_rows(core, cam), KG, d, dp=sib).start()
    for d in range(n_z):
        cam = (z - d + n_z) % n_z
        copy(final_rows(1 - core, cam), final_rows(1 - core, cam), KG, d, dp=sib).wait_recv()
    g_ref[...] = fin[...].astype(F32)

    for step in range(1, n_t):
        copy(w_ref.at[mine], w_all.at[tm, mine], KW, step, tm=peer(step)).wait_send()
        copy(w_part(step), w_part(step), KS, step, dp=sib).wait_send()
        copy(tok_ref, tok_all.at[tm], KT, step, tm=peer(step)).wait_send()
        copy(cot_ref, cot_all.at[tm], KC, step, tm=peer(step)).wait_send()
        head = (tm + step) % n_t
        copy(xa1.at[head], xb1.at[tm], KB1, step, tm=head).wait_send()
        copy(xa2.at[head], xb2.at[tm], KB2, step, tm=head).wait_send()
    for d in range(1, n_z):
        cam = (z + d) % n_z
        copy(p_send.at[cam], p_all.at[z], KP, d, view=cam).wait_send()
        copy(x1.at[cam], xa1.at[z], KX1, d, view=cam).wait_send()
        copy(x2.at[cam], xa2.at[z], KX2, d, view=cam).wait_send()
        copy(z_send.at[rows_of(cam)], z_recv.at[z], KZ, d, view=cam).wait_send()
        copy(final_rows(core, z), final_rows(core, z), KF, d, view=cam).wait_send()
    core_copy.wait_send()
    for s in range(1, n_y):
        copy(y_recv.at[yh], y_recv.at[yh], KY, s, dp=(dp + 2 * s) % n_d).wait_send()
    for d in range(n_z):
        cam = (z - d + n_z) % n_z
        copy(final_rows(core, cam), final_rows(core, cam), KG, d, dp=sib).wait_send()


def shards(n_d, n_z, n_t, tokens, cotangent, w_query, w_key, w_value, w_out, masks, rig_ids):
    rows, width = tokens.shape[2], tokens.shape[3]
    depth = w_query.shape[1]
    lanes = 2 * depth
    packed = jnp.concatenate([w_query, w_out.T, w_key, w_value], axis=1)
    vmem = pl.BlockSpec(memory_space=pltpu.VMEM)
    smem = pl.BlockSpec(memory_space=pltpu.SMEM)
    half_block = (n_z, rows, lanes)
    most = max(n_z, n_t, n_d)
    attended, grad_rows, grads = pl.pallas_call(
        functools.partial(kernel, n_d, n_z, n_t, depth),
        out_shape=(
            jax.ShapeDtypeStruct((rows, width), BF16),
            jax.ShapeDtypeStruct((rows, width), BF16),
            jax.ShapeDtypeStruct((2 * lanes, width), F32),
        ),
        in_specs=[vmem, vmem, vmem, smem, smem],
        out_specs=(vmem, vmem, vmem),
        scratch_shapes=[
            pltpu.VMEM((n_t, width, 2 * lanes), BF16),
            pltpu.VMEM((n_t, rows, width), BF16),
            pltpu.VMEM((n_t, rows, width), BF16),
            pltpu.VMEM((n_z, rows, 2 * lanes), BF16),
            pltpu.VMEM((n_z, rows, 2 * lanes), BF16),
            pltpu.VMEM((lanes, n_z * rows), BF16),
            pltpu.VMEM((n_z * rows, lanes), F32),
            pltpu.VMEM(half_block, BF16),
            pltpu.VMEM(half_block, BF16),
            pltpu.VMEM(half_block, BF16),
            pltpu.VMEM(half_block, BF16),
            pltpu.VMEM((n_t, rows, lanes), BF16),
            pltpu.VMEM((n_t, rows, lanes), BF16),
            pltpu.VMEM((2 * lanes, width), F32),
            pltpu.VMEM((lanes, width), BF16),
            pltpu.VMEM((lanes, width), BF16),
            pltpu.VMEM((lanes, width), BF16),
            pltpu.VMEM((n_z, lanes // n_z, width), BF16),
            pltpu.VMEM((n_d // 2, lanes // n_z, width), BF16),
            pltpu.VMEM((2 * lanes, width), BF16),
            pltpu.SemaphoreType.DMA((KINDS, most)),
            pltpu.SemaphoreType.DMA((KINDS, most)),
        ],
        compiler_params=pltpu.CompilerParams(
            collective_id=0, has_side_effects=True, vmem_limit_bytes=48 * 1024 * 1024
        ),
        cost_estimate=pl.CostEstimate(
            flops=3_000_000_000, bytes_accessed=8_000_000, transcendentals=1_000_000
        ),
    )(tokens.reshape(rows, width), cotangent.reshape(rows, width), packed, masks, rig_ids)
    return (
        attended.reshape(tokens.shape),
        grad_rows.reshape(tokens.shape),
        grads[:depth].T,
        grads[lanes:lanes + depth].T,
        grads[lanes + depth:].T,
        grads[depth:lanes],
    )


def solution(mesh):
    sizes = mesh.shape
    return jax.shard_map(
        functools.partial(shards, sizes["dp"], sizes["view"], sizes["tm"]),
        mesh=mesh,
        in_specs=(
            P("dp", "view", "tm", None),
            P("dp", "view", "tm", None),
            P(None, "tm"),
            P(None, "tm"),
            P(None, "tm"),
            P("tm", None),
            P(),
            P("dp"),
        ),
        out_specs=(
            P("dp", "view", "tm", None),
            P("dp", "view", "tm", None),
            P(None, "tm"),
            P(None, "tm"),
            P(None, "tm"),
            P("tm", None),
        ),
        check_vma=False,
    )
```

```python
import functools

import jax
import jax.numpy as jnp
from jax import lax
from jax.experimental import pallas as pl
from jax.experimental.pallas import tpu as pltpu
from jax.sharding import PartitionSpec as P

MESH = pl.DeviceIdType.MESH
BF16 = jnp.bfloat16
F32 = jnp.float32

(KW, KV1, KV2, KS1, KS2, KT1, KT2, KC1, KC2, KP, KX1, KX2, KB1, KB2, KR, KZ, KY, KF, KG) = range(19)
KINDS = 19

NT = (((1,), (1,)), ((), ()))


def dot(a, b):
    return jnp.dot(a, b, preferred_element_type=F32)


def dot_nt(a, b):
    return lax.dot_general(a, b, NT, preferred_element_type=F32)


def kernel(
    n_d, n_z, n_t, depth,
    tok_hbm, cot_hbm, wq_hbm, wk_hbm, wv_hbm, wo_hbm, masks_ref, rig_ref,
    att_ref, gtok_ref, g_ref,
    w_in, wo_in, w_all, tok_all, cot_all, p_send, p_all, kv_t, acc, x1, x2, xa1, xa2, xb1, xb2,
    g_sum, c_send, c_recv, z_send, z_recv, y_recv, fin,
    lsem, ssem, rsem,
):
    rows, width = tok_hbm.shape
    lanes = 2 * depth
    n_x = n_t // 2
    n_y = n_d // 2
    dp, z, tm = lax.axis_index("dp"), lax.axis_index("view"), lax.axis_index("tm")
    core, yh = dp % 2, dp // 2
    x, yl = tm // 2, tm % 2
    sib = dp + 1 - 2 * core
    pair = x * 2 + 1 - yl
    beyond = ((yh - 1 + 2 * yl + n_y) % n_y) * 2 + core

    loads = [
        pltpu.make_async_copy(src, dst, lsem.at[at])
        for at, (src, dst) in enumerate([
            (wq_hbm, w_in.at[0]), (wk_hbm, w_in.at[1]), (wv_hbm, w_in.at[2]), (wo_hbm, wo_in),
            (tok_hbm, tok_all.at[tm]), (cot_hbm, cot_all.at[tm]),
        ])
    ]
    for load in loads:
        load.start()

    def copy(src, dst, kind, at, **to):
        return pltpu.make_async_remote_copy(
            src_ref=src, dst_ref=dst, send_sem=ssem.at[kind, at], recv_sem=rsem.at[kind, at],
            device_id=to, device_id_type=MESH,
        )

    barrier = pltpu.get_barrier_semaphore()
    friends = [{"tm": (tm + s) % n_t} for s in range(1, n_t)]
    friends += [{"view": (z + s) % n_z} for s in range(1, n_z)]
    friends += [{"dp": (dp + 2 * s) % n_d} for s in range(1, n_y)]
    friends += [{"dp": sib}, {"dp": beyond, "tm": pair}]
    for friend in friends:
        pl.semaphore_signal(barrier, inc=1, device_id=friend, device_id_type=MESH)
    for load in loads[:4]:
        load.wait()
    w_all[tm, :, :lanes] = jnp.concatenate([w_in[0], wo_in[...].T], axis=1)
    w_all[tm, :, lanes:] = jnp.concatenate([w_in[1], w_in[2]], axis=1)
    pl.semaphore_wait(barrier, len(friends))

    def ahead(dx, side):
        return ((x + dx) % n_x) * 2 + side

    def behind(dx, side):
        return ((x - dx + n_x) % n_x) * 2 + side

    half, quarter = width // 2, width // 4

    def w_rows(head, start, size):
        return w_all.at[head, pl.ds(pl.multiple_of(start, size), size)]

    def w_mine(head):
        return w_rows(head, core * half, half)

    def w_along(dx):
        return copy(w_mine(tm), w_mine(tm), KW, dx, tm=ahead(dx, yl))

    def w_across(dx):
        head = behind(dx, yl)
        near = w_rows(head, core * half, quarter)
        far = w_rows(head, core * half + quarter, quarter)
        return copy(near, near, KV1, dx, tm=pair), copy(far, far, KV2, dx, dp=beyond, tm=pair)

    def w_share(dx, side, kind):
        part = w_mine(behind(dx, side))
        return copy(part, part, kind, dx, dp=sib)

    def w_shared(dx, side, kind):
        part = w_rows(behind(dx, side), (1 - core) * half, half)
        return copy(part, part, kind, dx, dp=sib)

    x_order = [1, 3, 2] if n_x == 4 else list(range(1, n_x))
    for dx in x_order:
        w_along(dx).start()
    for part in w_across(0):
        part.start()
    for load in loads[4:]:
        load.wait()

    first = lax.broadcasted_iota(jnp.int32, (rows, lanes), 1) < depth

    def project(head):
        both = dot(jnp.concatenate([tok_all[tm], cot_all[tm]], axis=0), w_all[head])
        p_send[head, :, :lanes] = jnp.where(first, both[:rows, :lanes], both[rows:, :lanes]).astype(BF16)
        p_send[head, :, lanes:] = both[:rows, lanes:].astype(BF16)

        @pl.when(head == z)
        def _():
            p_all[z] = p_send[head]

        @pl.when(head != z)
        def _():
            copy(p_send.at[head], p_all.at[z], KP, (head - z + n_z) % n_z, view=head).start()

    project(tm)
    for dx in x_order:
        copy(w_mine(behind(dx, yl)), w_mine(behind(dx, yl)), KW, dx, tm=ahead(dx, yl)).wait_recv()
        for part in w_across(dx):
            part.start()
        w_share(dx, yl, KS1).start()

    def cot_along(dx):
        return copy(cot_all.at[tm], cot_all.at[tm], KC1, dx, tm=ahead(dx, yl))

    for dx in x_order:
        cot_along(dx).start()

    def x_heads(i, _):
        dx = 1 + (i + z) % (n_x - 1)
        w_shared(dx, yl, KS1).wait_recv()
        project(behind(dx, yl))
        return 0

    if n_x > 1:
        lax.fori_loop(0, n_x - 1, x_heads, 0)
    for dx in [0] + x_order:
        head = behind(dx, 1 - yl)
        near = w_rows(head, core * half, quarter)
        far = w_rows(head, core * half + quarter, quarter)
        copy(near, near, KV1, dx, tm=pair).wait_recv()
        copy(far, far, KV2, dx, dp=beyond, tm=pair).wait_recv()
        w_share(dx, 1 - yl, KS2).start()

    def tok_pair():
        return copy(tok_all.at[tm], tok_all.at[tm], KT1, 0, tm=pair)

    def tok_along(dx, span, kind):
        return copy(tok_all.at[span], tok_all.at[span], kind, dx, tm=ahead(dx, yl))

    def cot_pair(dx):
        span = behind(dx, yl)
        return copy(cot_all.at[span], cot_all.at[span], KC2, dx, tm=pair)

    tok_pair().start()
    cot_pair(0).start()
    for dx in x_order:
        tok_along(dx, tm, KT1).start()

    def y_heads(i, _):
        dx = (i + z) % n_x
        w_shared(dx, 1 - yl, KS2).wait_recv()
        project(behind(dx, 1 - yl))
        return 0

    lax.fori_loop(0, n_x, y_heads, 0)

    def tok_forward():
        copy(tok_all.at[pair], tok_all.at[pair], KT1, 0, tm=pair).wait_recv()
        for dx in x_order:
            tok_along(dx, pair, KT2).start()

    def cot_forward():
        for dx in x_order:
            span = behind(dx, yl)
            copy(cot_all.at[span], cot_all.at[span], KC1, dx, tm=ahead(dx, yl)).wait_recv()
            cot_pair(dx).start()

    for d in range(1, n_z):
        copy(p_send.at[0], p_all.at[(z - d + n_z) % n_z], KP, d, view=(z + d) % n_z).wait_recv()
    tok_forward()

    total = n_z * rows
    kv_t[...] = p_all[:, :, lanes:].reshape(total, lanes).T
    acc[...] = jnp.zeros_like(acc)
    rig = rig_ref[0]
    factor = depth ** -0.5

    def attend(step, _):
        cam = (z + 1 + step) % n_z

        @pl.when(step == n_z // 2)
        def _():
            cot_forward()

        qd = p_all[cam, :, :lanes]
        zero = jnp.zeros_like(qd)
        block = jnp.concatenate([jnp.where(first, qd, zero), jnp.where(first, zero, qd)], axis=0)
        kv = p_all[:, :, lanes:].reshape(total, lanes)
        both = dot_nt(kv, block)
        scores = jnp.concatenate(
            [
                both[b * rows:(b + 1) * rows, :rows] * factor
                + (masks_ref[rig, cam, b] - 1).astype(F32) * 1e30
                for b in range(n_z)
            ],
            axis=0,
        )
        weights = jnp.exp(scores - jnp.max(scores, axis=0, keepdims=True))
        probs = weights * (1.0 / jnp.sum(weights, axis=0, keepdims=True))
        probs_half = probs.astype(BF16)
        attn = dot(kv_t[depth:], probs_half)
        grad_attn = qd.astype(F32).T[depth:]
        delta = jnp.sum(grad_attn * attn.astype(BF16).astype(F32), axis=0, keepdims=True)
        dscore = (probs * (both[:, rows:] - delta) * factor).astype(BF16)
        dq = dot(kv_t[:depth], dscore)
        x1[cam] = jnp.concatenate([dq, attn], axis=0).T.astype(BF16)

        @pl.when(cam == z)
        def _():
            xa1[z] = x1[cam]

        @pl.when(cam != z)
        def _():
            copy(x1.at[cam], xa1.at[z], KX1, (cam - z + n_z) % n_z, view=cam).start()

        part = dot(jnp.concatenate([dscore, probs_half], axis=1), block)
        acc[...] += part.astype(BF16).astype(F32)
        return 0

    lax.fori_loop(0, n_z, attend, 0)
    x2[...] = acc[...].astype(BF16).reshape(n_z, rows, lanes)
    for d in range(1, n_z):
        cam = (z + d) % n_z
        copy(x2.at[cam], xa2.at[z], KX2, d, view=cam).start()
    xa2[z] = x2[z]

    def hand_on(src, dst, kind, head):
        @pl.when(head == tm)
        def _():
            dst[tm] = src[head]

        @pl.when(head != tm)
        def _():
            copy(src.at[head], dst.at[tm], kind, (head - tm + n_t) % n_t, tm=head).start()

    def arrive1(d, _):
        head = (z - d + n_z) % n_z

        @pl.when(d > 0)
        def _():
            copy(xa1.at[head], xa1.at[head], KX1, d, view=head).wait_recv()

        hand_on(xa1, xb1, KB1, head)
        return 0

    def arrive2(d, _):
        head = (z - d + n_z) % n_z

        @pl.when(d > 0)
        def _():
            copy(xa2.at[head], xa2.at[head], KX2, d, view=head).wait_recv()

        hand_on(xa2, xb2, KB2, head)
        return 0

    lax.fori_loop(0, n_z, lambda i, _: arrive1((i + tm) % n_z, _), 0)
    lax.fori_loop(0, n_z, lambda i, _: arrive2((i + tm) % n_z, _), 0)

    for f in range(1, n_t):
        span = (tm - f + n_t) % n_t
        copy(xb1.at[span], xb1.at[span], KB1, f, tm=span).wait_recv()
        copy(xb2.at[span], xb2.at[span], KB2, f, tm=span).wait_recv()
    for dx in x_order:
        span, other = behind(dx, yl), behind(dx, 1 - yl)
        copy(tok_all.at[span], tok_all.at[span], KT1, dx, tm=ahead(dx, yl)).wait_recv()
        copy(tok_all.at[other], tok_all.at[other], KT2, dx, tm=ahead(dx, yl)).wait_recv()
    for dx in [0] + x_order:
        other = behind(dx, 1 - yl)
        copy(cot_all.at[other], cot_all.at[other], KC2, dx, tm=pair).wait_recv()

    b1 = xb1[...].reshape(n_t * rows, lanes).T
    b2 = xb2[...].reshape(n_t * rows, lanes).T
    tokens = tok_all[...].reshape(n_t * rows, width)
    cots = cot_all[...].reshape(n_t * rows, width)
    g_sum[:depth] = dot(b1[:depth], tokens)
    g_sum[depth:lanes] = dot(b1[depth:], cots)
    g_sum[lanes:] = dot(b2, tokens)

    keep = pl.ds(pl.multiple_of(core * lanes, lanes), lanes)
    give = pl.ds(pl.multiple_of((1 - core) * lanes, lanes), lanes)
    c_send[...] = g_sum[give].astype(BF16)
    core_copy = copy(c_send, c_recv, KR, 0, dp=sib)
    core_copy.start()
    core_copy.wait_recv()
    g_sum[keep] = g_sum[keep] + c_recv[...].astype(F32)
    z_send[...] = g_sum[keep].astype(BF16)

    chunk = lanes // n_z

    def rows_of(index):
        return pl.ds(pl.multiple_of(index * chunk, chunk), chunk)

    for d in range(1, n_z):
        cam = (z + d) % n_z
        copy(z_send.at[rows_of(cam)], z_recv.at[z], KZ, d, view=cam).start()

    def finish(head, sums):
        one, two = xa1[head], xa2[head]
        zero = jnp.zeros_like(one)
        left = jnp.concatenate(
            [
                jnp.concatenate([jnp.where(first, one, zero), two], axis=1),
                jnp.concatenate([jnp.where(first, zero, one), zero], axis=1),
            ],
            axis=0,
        )
        return sums + dot_nt(left, w_all[head])

    sums = lax.fori_loop(0, n_z, finish, jnp.zeros((2 * rows, width), F32))
    gtok_ref[...] = sums[:rows].astype(BF16)
    att_ref[...] = sums[rows:].astype(BF16)

    chunk_sum = z_send[rows_of(z)].astype(F32)
    for d in range(1, n_z):
        cam = (z - d + n_z) % n_z
        copy(z_recv.at[cam], z_recv.at[cam], KZ, d, view=cam).wait_recv()
        chunk_sum = chunk_sum + z_recv[cam].astype(F32)
    y_recv[yh] = chunk_sum.astype(BF16)

    for s in range(1, n_y):
        copy(y_recv.at[yh], y_recv.at[yh], KY, s, dp=(dp + 2 * s) % n_d).start()
    for s in range(1, n_y):
        other = (yh - s + n_y) % n_y
        copy(y_recv.at[other], y_recv.at[other], KY, s, dp=(dp + 2 * s) % n_d).wait_recv()
    all_sum = y_recv[0].astype(F32)
    for s in range(1, n_y):
        all_sum = all_sum + y_recv[s].astype(F32)

    def final_rows(side, index):
        return fin.at[pl.ds(pl.multiple_of(side * lanes + index * chunk, chunk), chunk)]

    fin[pl.ds(pl.multiple_of(core * lanes + z * chunk, chunk), chunk)] = all_sum.astype(BF16)
    for d in range(1, n_z):
        copy(final_rows(core, z), final_rows(core, z), KF, d, view=(z + d) % n_z).start()
    copy(final_rows(core, z), final_rows(core, z), KG, 0, dp=sib).start()
    for d in range(1, n_z):
        cam = (z - d + n_z) % n_z
        copy(final_rows(core, cam), final_rows(core, cam), KF, d, view=cam).wait_recv()
        copy(final_rows(core, cam), final_rows(core, cam), KG, d, dp=sib).start()
    for d in range(n_z):
        cam = (z - d + n_z) % n_z
        copy(final_rows(1 - core, cam), final_rows(1 - core, cam), KG, d, dp=sib).wait_recv()
    g_ref[...] = fin[...].astype(F32)

    for dx in [0] + x_order:
        gone = [*w_across(dx), w_share(dx, 1 - yl, KS2), cot_pair(dx)]
        if dx:
            gone += [w_along(dx), w_share(dx, yl, KS1), cot_along(dx)]
            gone += [tok_along(dx, tm, KT1), tok_along(dx, pair, KT2)]
        else:
            gone += [tok_pair()]
        for one in gone:
            one.wait_send()
    for step in range(1, n_t):
        head = (tm + step) % n_t
        copy(xa1.at[head], xb1.at[tm], KB1, step, tm=head).wait_send()
        copy(xa2.at[head], xb2.at[tm], KB2, step, tm=head).wait_send()
    for d in range(1, n_z):
        cam = (z + d) % n_z
        copy(p_send.at[cam], p_all.at[z], KP, d, view=cam).wait_send()
        copy(x1.at[cam], xa1.at[z], KX1, d, view=cam).wait_send()
        copy(x2.at[cam], xa2.at[z], KX2, d, view=cam).wait_send()
        copy(z_send.at[rows_of(cam)], z_recv.at[z], KZ, d, view=cam).wait_send()
        copy(final_rows(core, z), final_rows(core, z), KF, d, view=cam).wait_send()
    core_copy.wait_send()
    for s in range(1, n_y):
        copy(y_recv.at[yh], y_recv.at[yh], KY, s, dp=(dp + 2 * s) % n_d).wait_send()
    for d in range(n_z):
        cam = (z - d + n_z) % n_z
        copy(final_rows(core, cam), final_rows(core, cam), KG, d, dp=sib).wait_send()


def shards(n_d, n_z, n_t, tokens, cotangent, w_query, w_key, w_value, w_out, masks, rig_ids):
    rows, width = tokens.shape[2], tokens.shape[3]
    depth = w_query.shape[1]
    lanes = 2 * depth
    vmem = pl.BlockSpec(memory_space=pltpu.VMEM)
    smem = pl.BlockSpec(memory_space=pltpu.SMEM)
    hbm = pl.BlockSpec(memory_space=pl.ANY)
    half_block = (n_z, rows, lanes)
    most = max(n_z, n_t, n_d)
    attended, grad_rows, grads = pl.pallas_call(
        functools.partial(kernel, n_d, n_z, n_t, depth),
        out_shape=(
            jax.ShapeDtypeStruct((rows, width), BF16),
            jax.ShapeDtypeStruct((rows, width), BF16),
            jax.ShapeDtypeStruct((2 * lanes, width), F32),
        ),
        in_specs=[hbm] * 6 + [smem] * 2,
        out_specs=(vmem, vmem, vmem),
        scratch_shapes=[
            pltpu.VMEM((3, width, depth), BF16),
            pltpu.VMEM((depth, width), BF16),
            pltpu.VMEM((n_t, width, 2 * lanes), BF16),
            pltpu.VMEM((n_t, rows, width), BF16),
            pltpu.VMEM((n_t, rows, width), BF16),
            pltpu.VMEM((n_z, rows, 2 * lanes), BF16),
            pltpu.VMEM((n_z, rows, 2 * lanes), BF16),
            pltpu.VMEM((lanes, n_z * rows), BF16),
            pltpu.VMEM((n_z * rows, lanes), F32),
            pltpu.VMEM(half_block, BF16),
            pltpu.VMEM(half_block, BF16),
            pltpu.VMEM(half_block, BF16),
            pltpu.VMEM(half_block, BF16),
            pltpu.VMEM((n_t, rows, lanes), BF16),
            pltpu.VMEM((n_t, rows, lanes), BF16),
            pltpu.VMEM((2 * lanes, width), F32),
            pltpu.VMEM((lanes, width), BF16),
            pltpu.VMEM((lanes, width), BF16),
            pltpu.VMEM((lanes, width), BF16),
            pltpu.VMEM((n_z, lanes // n_z, width), BF16),
            pltpu.VMEM((n_d // 2, lanes // n_z, width), BF16),
            pltpu.VMEM((2 * lanes, width), BF16),
            pltpu.SemaphoreType.DMA((6,)),
            pltpu.SemaphoreType.DMA((KINDS, most)),
            pltpu.SemaphoreType.DMA((KINDS, most)),
        ],
        compiler_params=pltpu.CompilerParams(
            collective_id=0, has_side_effects=True, vmem_limit_bytes=48 * 1024 * 1024
        ),
        cost_estimate=pl.CostEstimate(
            flops=3_000_000_000, bytes_accessed=8_000_000, transcendentals=1_000_000
        ),
    )(tokens.reshape(rows, width), cotangent.reshape(rows, width), w_query, w_key, w_value, w_out,
      masks, rig_ids)
    return (
        attended.reshape(tokens.shape),
        grad_rows.reshape(tokens.shape),
        grads[:depth].T,
        grads[lanes:lanes + depth].T,
        grads[lanes + depth:].T,
        grads[depth:lanes],
    )


def solution(mesh):
    sizes = mesh.shape
    return jax.shard_map(
        functools.partial(shards, sizes["dp"], sizes["view"], sizes["tm"]),
        mesh=mesh,
        in_specs=(
            P("dp", "view", "tm", None),
            P("dp", "view", "tm", None),
            P(None, "tm"),
            P(None, "tm"),
            P(None, "tm"),
            P("tm", None),
            P(),
            P("dp"),
        ),
        out_specs=(
            P("dp", "view", "tm", None),
            P("dp", "view", "tm", None),
            P(None, "tm"),
            P(None, "tm"),
            P(None, "tm"),
            P("tm", None),
        ),
        check_vma=False,
    )
```

```python
import functools

import jax
import jax.numpy as jnp
from jax import lax
from jax.experimental import pallas as pl
from jax.experimental.pallas import tpu as pltpu
from jax.sharding import PartitionSpec as P

MESH = pl.DeviceIdType.MESH
BF16 = jnp.bfloat16
F32 = jnp.float32

(KW, KV1, KV2, KS1, KS2, KT1, KT2, KC1, KC2, KP, KX1, KX2, KB1, KB2, KR, KZ, KY, KF, KG) = range(19)
KINDS = 19

NT = (((1,), (1,)), ((), ()))


def dot(a, b):
    return jnp.dot(a, b, preferred_element_type=F32)


def dot_nt(a, b):
    return lax.dot_general(a, b, NT, preferred_element_type=F32)


def kernel(
    n_d, n_z, n_t, depth,
    tok_hbm, cot_hbm, wq_hbm, wk_hbm, wv_hbm, wo_hbm, masks_ref, rig_ref,
    att_ref, gtok_ref, g_ref,
    w_all, tok_all, cot_all, p_send, p_all, kv_t, pairs, x1, x2, xa1, xa2, xb1, xb2,
    g_sum, c_send, c_recv, z_send, z_recv, y_recv, fin,
    lsem, ssem, rsem,
):
    rows, width = tok_hbm.shape
    lanes = 2 * depth
    n_x = n_t // 2
    n_y = n_d // 2
    dp, z, tm = lax.axis_index("dp"), lax.axis_index("view"), lax.axis_index("tm")
    core, yh = dp % 2, dp // 2
    x, yl = tm // 2, tm % 2
    sib = dp + 1 - 2 * core
    pair = x * 2 + 1 - yl
    beyond = ((yh - 1 + 2 * yl + n_y) % n_y) * 2 + core

    loads = [
        pltpu.make_async_copy(src, dst, lsem.at[at])
        for at, (src, dst) in enumerate([
            (wq_hbm, w_all.at[tm, pl.ds(0, depth)]), (wo_hbm, w_all.at[tm, pl.ds(depth, depth)]),
            (wk_hbm, w_all.at[tm, pl.ds(lanes, depth)]),
            (wv_hbm, w_all.at[tm, pl.ds(lanes + depth, depth)]),
            (tok_hbm, tok_all.at[tm]), (cot_hbm, cot_all.at[tm]),
        ])
    ]
    for load in loads:
        load.start()

    def copy(src, dst, kind, at, **to):
        return pltpu.make_async_remote_copy(
            src_ref=src, dst_ref=dst, send_sem=ssem.at[kind, at], recv_sem=rsem.at[kind, at],
            device_id=to, device_id_type=MESH,
        )

    barrier = pltpu.get_barrier_semaphore()
    friends = [{"tm": (tm + s) % n_t} for s in range(1, n_t)]
    friends += [{"view": (z + s) % n_z} for s in range(1, n_z)]
    friends += [{"dp": (dp + 2 * s) % n_d} for s in range(1, n_y)]
    friends += [{"dp": sib}, {"dp": beyond, "tm": pair}]
    for friend in friends:
        pl.semaphore_signal(barrier, inc=1, device_id=friend, device_id_type=MESH)
    for load in loads:
        load.wait()
    pl.semaphore_wait(barrier, len(friends))

    def ahead(dx, side):
        return ((x + dx) % n_x) * 2 + side

    def behind(dx, side):
        return ((x - dx + n_x) % n_x) * 2 + side

    half, quarter = lanes, depth

    def w_rows(head, start, size):
        return w_all.at[head, pl.ds(pl.multiple_of(start, size), size)]

    def w_mine(head):
        return w_rows(head, core * half, half)

    def w_along(dx):
        return copy(w_mine(tm), w_mine(tm), KW, dx, tm=ahead(dx, yl))

    def w_across(dx):
        head = behind(dx, yl)
        near = w_rows(head, core * half, quarter)
        far = w_rows(head, core * half + quarter, quarter)
        return copy(near, near, KV1, dx, tm=pair), copy(far, far, KV2, dx, dp=beyond, tm=pair)

    def w_share(dx, side, kind):
        part = w_mine(behind(dx, side))
        return copy(part, part, kind, dx, dp=sib)

    def w_shared(dx, side, kind):
        part = w_rows(behind(dx, side), (1 - core) * half, half)
        return copy(part, part, kind, dx, dp=sib)

    x_order = [1, 3, 2] if n_x == 4 else list(range(1, n_x))
    for dx in x_order:
        w_along(dx).start()
    for part in w_across(0):
        part.start()

    def tok_pair():
        return copy(tok_all.at[tm], tok_all.at[tm], KT1, 0, tm=pair)

    def tok_along(dx, span, kind):
        return copy(tok_all.at[span], tok_all.at[span], kind, dx, tm=ahead(dx, yl))

    def cot_pair(dx):
        span = behind(dx, yl)
        return copy(cot_all.at[span], cot_all.at[span], KC2, dx, tm=pair)

    def cot_along(dx):
        return copy(cot_all.at[tm], cot_all.at[tm], KC1, dx, tm=ahead(dx, yl))

    tok_pair().start()

    first = lax.broadcasted_iota(jnp.int32, (rows, lanes), 1) < depth

    def project(head):
        both = dot_nt(jnp.concatenate([tok_all[tm], cot_all[tm]], axis=0), w_all[head])
        p_send[head, :, :lanes] = jnp.where(first, both[:rows, :lanes], both[rows:, :lanes]).astype(BF16)
        p_send[head, :, lanes:] = both[:rows, lanes:].astype(BF16)

        @pl.when(head == z)
        def _():
            p_all[z] = p_send[head]

        @pl.when(head != z)
        def _():
            copy(p_send.at[head], p_all.at[z], KP, (head - z + n_z) % n_z, view=head).start()

    project(tm)
    for dx in x_order:
        copy(w_mine(behind(dx, yl)), w_mine(behind(dx, yl)), KW, dx, tm=ahead(dx, yl)).wait_recv()
        for part in w_across(dx):
            part.start()
        w_share(dx, yl, KS1).start()

    for dx in x_order:
        cot_along(dx).start()

    def x_heads(i, _):
        dx = 1 + (i + z) % (n_x - 1)
        w_shared(dx, yl, KS1).wait_recv()
        project(behind(dx, yl))
        return 0

    if n_x > 1:
        lax.fori_loop(0, n_x - 1, x_heads, 0)
    for dx in [0] + x_order:
        head = behind(dx, 1 - yl)
        near = w_rows(head, core * half, quarter)
        far = w_rows(head, core * half + quarter, quarter)
        copy(near, near, KV1, dx, tm=pair).wait_recv()
        copy(far, far, KV2, dx, dp=beyond, tm=pair).wait_recv()
        w_share(dx, 1 - yl, KS2).start()

    cot_pair(0).start()
    for dx in x_order:
        tok_along(dx, tm, KT1).start()

    def y_heads(i, _):
        dx = (i + z) % n_x
        w_shared(dx, 1 - yl, KS2).wait_recv()
        project(behind(dx, 1 - yl))
        return 0

    lax.fori_loop(0, n_x, y_heads, 0)

    def tok_forward():
        copy(tok_all.at[pair], tok_all.at[pair], KT1, 0, tm=pair).wait_recv()
        for dx in x_order:
            tok_along(dx, pair, KT2).start()

    def cot_forward():
        for dx in x_order:
            span = behind(dx, yl)
            copy(cot_all.at[span], cot_all.at[span], KC1, dx, tm=ahead(dx, yl)).wait_recv()
            cot_pair(dx).start()

    for d in range(1, n_z):
        copy(p_send.at[0], p_all.at[(z - d + n_z) % n_z], KP, d, view=(z + d) % n_z).wait_recv()
    tok_forward()

    total = n_z * rows
    kv_t[...] = p_all[:, :, lanes:].reshape(total, lanes).T
    rig = rig_ref[0]
    factor = depth ** -0.5

    def split(cam):
        qd = p_all[cam, :, :lanes]
        zero = jnp.zeros_like(qd)
        return jnp.where(first, qd, zero), jnp.where(first, zero, qd)

    def attend(step, _):
        cams = [(z + 1 + 2 * step) % n_z, (z + 2 + 2 * step) % n_z]

        @pl.when(step == 1)
        def _():
            cot_forward()

        query0, grad0 = split(cams[0])
        query1, grad1 = split(cams[1])
        kv = p_all[:, :, lanes:].reshape(total, lanes)
        both = dot_nt(kv, jnp.concatenate([query0, query1, grad0, grad1], axis=0))
        scores = jnp.concatenate(
            [
                jnp.concatenate(
                    [
                        both[b * rows:(b + 1) * rows, q * rows:(q + 1) * rows] * factor
                        + (masks_ref[rig, cams[q], b] - 1).astype(F32) * 1e30
                        for q in range(2)
                    ],
                    axis=1,
                )
                for b in range(n_z)
            ],
            axis=0,
        )
        weights = jnp.exp(scores - jnp.max(scores, axis=0, keepdims=True))
        probs = weights * (1.0 / jnp.sum(weights, axis=0, keepdims=True))
        probs_half = probs.astype(BF16)
        attn = dot(kv_t[depth:], probs_half)
        grad_attn = jnp.concatenate(
            [(query0 + grad0).astype(F32).T[depth:], (query1 + grad1).astype(F32).T[depth:]], axis=1
        )
        delta = jnp.sum(grad_attn * attn.astype(BF16).astype(F32), axis=0, keepdims=True)
        dscore = (probs * (both[:, 2 * rows:] - delta) * factor).astype(BF16)
        dq = dot(kv_t[:depth], dscore)
        out = jnp.concatenate([dq, attn], axis=0)
        for q, cam in enumerate(cams):
            cols = slice(q * rows, (q + 1) * rows)
            x1[cam] = out[:, cols].T.astype(BF16)

            @pl.when(cam == z)
            def _():
                xa1[z] = x1[cam]

            @pl.when(cam != z)
            def _():
                copy(x1.at[cam], xa1.at[z], KX1, (cam - z + n_z) % n_z, view=cam).start()

            pairs[cam, :, :rows] = dscore[:, cols]
            pairs[cam, :, rows:] = probs_half[:, cols]
        return 0

    lax.fori_loop(0, n_z // 2, attend, 0)

    def keys(step, _):
        cams = [(z + 1 + 2 * step) % n_z, (z + 2 + 2 * step) % n_z]
        sums = jnp.zeros((2 * rows, lanes), F32)
        for query in range(n_z):
            block = jnp.concatenate(split(query), axis=0)
            left = jnp.concatenate(
                [pairs[query, pl.ds(pl.multiple_of(cam * rows, rows), rows)] for cam in cams], axis=0
            )
            sums = sums + dot(left, block).astype(BF16).astype(F32)
        for k, cam in enumerate(cams):
            x2[cam] = sums[k * rows:(k + 1) * rows].astype(BF16)

            @pl.when(cam == z)
            def _():
                xa2[z] = x2[cam]

            @pl.when(cam != z)
            def _():
                copy(x2.at[cam], xa2.at[z], KX2, (cam - z + n_z) % n_z, view=cam).start()
        return 0

    lax.fori_loop(0, n_z // 2, keys, 0)

    def hand_on(src, dst, kind, head):
        @pl.when(head == tm)
        def _():
            dst[tm] = src[head]

        @pl.when(head != tm)
        def _():
            copy(src.at[head], dst.at[tm], kind, (head - tm + n_t) % n_t, tm=head).start()

    def arrive1(d, _):
        head = (z - d + n_z) % n_z

        @pl.when(d > 0)
        def _():
            copy(xa1.at[head], xa1.at[head], KX1, d, view=head).wait_recv()

        hand_on(xa1, xb1, KB1, head)
        return 0

    def arrive2(d, _):
        head = (z - d + n_z) % n_z

        @pl.when(d > 0)
        def _():
            copy(xa2.at[head], xa2.at[head], KX2, d, view=head).wait_recv()

        hand_on(xa2, xb2, KB2, head)
        return 0

    lax.fori_loop(0, n_z, lambda i, _: arrive1((i + tm) % n_z, _), 0)
    lax.fori_loop(0, n_z, lambda i, _: arrive2((i + tm) % n_z, _), 0)

    def handed(ref, kind):
        for f in range(1, n_t):
            span = (tm - f + n_t) % n_t
            copy(ref.at[span], ref.at[span], kind, f, tm=span).wait_recv()

    chunk = width // n_z
    keep = pl.multiple_of(core * depth, depth)
    give = pl.multiple_of((1 - core) * depth, depth)

    def core_copy(p):
        return copy(c_send.at[p], c_recv.at[p], KR, p, dp=sib)

    def camera_copy(p, d):
        cam = (z + d) % n_z
        return copy(z_send.at[p, cam], z_recv.at[p, z], KZ, p * n_z + d, view=cam)

    def clip_copy(p, s):
        part = y_recv.at[p, yh]
        return copy(part, part, KY, p * n_y + s, dp=(dp + 2 * s) % n_d)

    def final_copy(p, d):
        part = fin.at[p, core, z]
        return copy(part, part, KF, p * n_z + d, view=(z + d) % n_z)

    def final_share(p, d):
        part = fin.at[p, core, (z - d + n_z) % n_z]
        return copy(part, part, KG, p * n_z + d, dp=sib)

    def core_start(p):
        c_send[p] = g_sum[p, pl.ds(give, depth)].astype(BF16)
        core_copy(p).start()

    def camera_start(p):
        core_copy(p).wait_recv()
        total = (g_sum[p, pl.ds(keep, depth)] + c_recv[p].astype(F32)).astype(BF16)
        for cam in range(n_z):
            z_send[p, cam] = total[:, cam * chunk:(cam + 1) * chunk]
        for d in range(1, n_z):
            camera_copy(p, d).start()

    def clip_start(p):
        total = z_send[p, z].astype(F32)
        for d in range(1, n_z):
            cam = (z - d + n_z) % n_z
            copy(z_recv.at[p, cam], z_recv.at[p, cam], KZ, p * n_z + d, view=cam).wait_recv()
            total = total + z_recv[p, cam].astype(F32)
        y_recv[p, yh] = total.astype(BF16)
        for s in range(1, n_y):
            clip_copy(p, s).start()

    def spread_start(p):
        for s in range(1, n_y):
            other = y_recv.at[p, (yh - s + n_y) % n_y]
            copy(other, other, KY, p * n_y + s, dp=(dp + 2 * s) % n_d).wait_recv()
        total = y_recv[p, 0].astype(F32)
        for s in range(1, n_y):
            total = total + y_recv[p, s].astype(F32)
        fin[p, core, z] = total.astype(BF16)
        for d in range(1, n_z):
            final_copy(p, d).start()
        final_share(p, 0).start()

    def spread_forward(p):
        for d in range(1, n_z):
            part = fin.at[p, core, (z - d + n_z) % n_z]
            copy(part, part, KF, p * n_z + d, view=(z + d) % n_z).wait_recv()
            final_share(p, d).start()

    def spread_end(p):
        for d in range(n_z):
            part = fin.at[p, 1 - core, (z - d + n_z) % n_z]
            copy(part, part, KG, p * n_z + d, dp=sib).wait_recv()
        for side in range(2):
            for cam in range(n_z):
                place = (slice((2 * p + side) * depth, (2 * p + side + 1) * depth),
                         slice(cam * chunk, (cam + 1) * chunk))
                g_ref[place] = fin[p, side, cam].astype(F32)

    def finish(head, sums):
        one, two = xa1[head], xa2[head]
        zero = jnp.zeros_like(one)
        left = jnp.concatenate(
            [
                jnp.concatenate([jnp.where(first, one, zero), two], axis=1),
                jnp.concatenate([jnp.where(first, zero, one), zero], axis=1),
            ],
            axis=0,
        )
        return sums + dot(left, w_all[head])

    for dx in x_order:
        span, other = behind(dx, yl), behind(dx, 1 - yl)
        copy(tok_all.at[span], tok_all.at[span], KT1, dx, tm=ahead(dx, yl)).wait_recv()
        copy(tok_all.at[other], tok_all.at[other], KT2, dx, tm=ahead(dx, yl)).wait_recv()
    for dx in [0] + x_order:
        other = behind(dx, 1 - yl)
        copy(cot_all.at[other], cot_all.at[other], KC2, dx, tm=pair).wait_recv()
    tokens = tok_all[...].reshape(n_t * rows, width)
    cots = cot_all[...].reshape(n_t * rows, width)
    handed(xb1, KB1)
    b1 = xb1[...].reshape(n_t * rows, lanes).T
    g_sum[0, :depth] = dot(b1[:depth], tokens)
    g_sum[0, depth:] = dot(b1[depth:], cots)
    core_start(0)
    handed(xb2, KB2)
    g_sum[1] = dot(xb2[...].reshape(n_t * rows, lanes).T, tokens)
    camera_start(0)
    core_start(1)
    camera_start(1)
    sums = lax.fori_loop(0, n_z // 2, finish, jnp.zeros((2 * rows, width), F32))
    clip_start(0)
    sums = lax.fori_loop(n_z // 2, n_z, finish, sums)
    gtok_ref[...] = sums[:rows].astype(BF16)
    att_ref[...] = sums[rows:].astype(BF16)
    clip_start(1)
    spread_start(0)
    spread_start(1)
    spread_forward(0)
    spread_end(0)
    spread_forward(1)
    spread_end(1)

    for dx in [0] + x_order:
        gone = [*w_across(dx), w_share(dx, 1 - yl, KS2), cot_pair(dx)]
        if dx:
            gone += [w_along(dx), w_share(dx, yl, KS1), cot_along(dx)]
            gone += [tok_along(dx, tm, KT1), tok_along(dx, pair, KT2)]
        else:
            gone += [tok_pair()]
        for one in gone:
            one.wait_send()
    for step in range(1, n_t):
        head = (tm + step) % n_t
        copy(xa1.at[head], xb1.at[tm], KB1, step, tm=head).wait_send()
        copy(xa2.at[head], xb2.at[tm], KB2, step, tm=head).wait_send()
    for d in range(1, n_z):
        cam = (z + d) % n_z
        copy(p_send.at[cam], p_all.at[z], KP, d, view=cam).wait_send()
        copy(x1.at[cam], xa1.at[z], KX1, d, view=cam).wait_send()
        copy(x2.at[cam], xa2.at[z], KX2, d, view=cam).wait_send()
    for p in range(2):
        core_copy(p).wait_send()
        for d in range(1, n_z):
            camera_copy(p, d).wait_send()
            final_copy(p, d).wait_send()
        for s in range(1, n_y):
            clip_copy(p, s).wait_send()
        for d in range(n_z):
            final_share(p, d).wait_send()


def shards(n_d, n_z, n_t, tokens, cotangent, w_query, w_key, w_value, w_out, masks, rig_ids):
    rows, width = tokens.shape[2], tokens.shape[3]
    depth = w_query.shape[1]
    lanes = 2 * depth
    vmem = pl.BlockSpec(memory_space=pltpu.VMEM)
    smem = pl.BlockSpec(memory_space=pltpu.SMEM)
    hbm = pl.BlockSpec(memory_space=pl.ANY)
    half_block = (n_z, rows, lanes)
    most = 2 * max(n_z, n_t, n_d)
    attended, grad_rows, grads = pl.pallas_call(
        functools.partial(kernel, n_d, n_z, n_t, depth),
        out_shape=(
            jax.ShapeDtypeStruct((rows, width), BF16),
            jax.ShapeDtypeStruct((rows, width), BF16),
            jax.ShapeDtypeStruct((2 * lanes, width), F32),
        ),
        in_specs=[hbm] * 6 + [smem] * 2,
        out_specs=(vmem, vmem, vmem),
        scratch_shapes=[
            pltpu.VMEM((n_t, 2 * lanes, width), BF16),
            pltpu.VMEM((n_t, rows, width), BF16),
            pltpu.VMEM((n_t, rows, width), BF16),
            pltpu.VMEM((n_z, rows, 2 * lanes), BF16),
            pltpu.VMEM((n_z, rows, 2 * lanes), BF16),
            pltpu.VMEM((lanes, n_z * rows), BF16),
            pltpu.VMEM((n_z, n_z * rows, 2 * rows), BF16),
            pltpu.VMEM(half_block, BF16),
            pltpu.VMEM(half_block, BF16),
            pltpu.VMEM(half_block, BF16),
            pltpu.VMEM(half_block, BF16),
            pltpu.VMEM((n_t, rows, lanes), BF16),
            pltpu.VMEM((n_t, rows, lanes), BF16),
            pltpu.VMEM((2, lanes, width), F32),
            pltpu.VMEM((2, depth, width), BF16),
            pltpu.VMEM((2, depth, width), BF16),
            pltpu.VMEM((2, n_z, depth, width // n_z), BF16),
            pltpu.VMEM((2, n_z, depth, width // n_z), BF16),
            pltpu.VMEM((2, n_d // 2, depth, width // n_z), BF16),
            pltpu.VMEM((2, 2, n_z, depth, width // n_z), BF16),
            pltpu.SemaphoreType.DMA((6,)),
            pltpu.SemaphoreType.DMA((KINDS, most)),
            pltpu.SemaphoreType.DMA((KINDS, most)),
        ],
        compiler_params=pltpu.CompilerParams(
            collective_id=0, has_side_effects=True, vmem_limit_bytes=48 * 1024 * 1024
        ),
        cost_estimate=pl.CostEstimate(
            flops=3_000_000_000, bytes_accessed=8_000_000, transcendentals=1_000_000
        ),
    )(tokens.reshape(rows, width), cotangent.reshape(rows, width), w_query.T, w_key.T, w_value.T, w_out,
      masks, rig_ids)
    return (
        attended.reshape(tokens.shape),
        grad_rows.reshape(tokens.shape),
        grads[:depth].T,
        grads[lanes:lanes + depth].T,
        grads[lanes + depth:].T,
        grads[depth:lanes],
    )


def solution(mesh):
    sizes = mesh.shape
    return jax.shard_map(
        functools.partial(shards, sizes["dp"], sizes["view"], sizes["tm"]),
        mesh=mesh,
        in_specs=(
            P("dp", "view", "tm", None),
            P("dp", "view", "tm", None),
            P(None, "tm"),
            P(None, "tm"),
            P(None, "tm"),
            P("tm", None),
            P(),
            P("dp"),
        ),
        out_specs=(
            P("dp", "view", "tm", None),
            P("dp", "view", "tm", None),
            P(None, "tm"),
            P(None, "tm"),
            P(None, "tm"),
            P("tm", None),
        ),
        check_vma=False,
    )
```

```python
import functools

import jax
import jax.numpy as jnp
from jax import lax
from jax.experimental import pallas as pl
from jax.experimental.pallas import tpu as pltpu
from jax.sharding import PartitionSpec as P

MESH = pl.DeviceIdType.MESH
BF16 = jnp.bfloat16
F32 = jnp.float32

(KW, KV, KS1, KS2, KT1, KT2, KC1, KC2, KP, KQ, KX1, KX2, KB1, KB2, KR, KZ, KY, KF, KG) = range(19)
KINDS = 19

NT = (((1,), (1,)), ((), ()))


def dot(a, b):
    return jnp.dot(a, b, preferred_element_type=F32)


def dot_nt(a, b):
    return lax.dot_general(a, b, NT, preferred_element_type=F32)


def kernel(
    n_d, n_z, n_t, depth,
    tok_hbm, cot_hbm, wq_hbm, wk_hbm, wv_hbm, wo_hbm, masks_ref, rig_ref,
    both_hbm, g_ref,
    w_all, tok_all, cot_all, p_send, p_all, kv_t, pairs, x1, x2, xa1, xa2, xb1, xb2,
    g_sum, c_send, c_recv, z_send, z_recv, y_recv, fin, both_out,
    lsem, ssem, rsem,
):
    rows, width = tok_hbm.shape
    lanes = 2 * depth
    n_x = n_t // 2
    n_y = n_d // 2
    dp, z, tm = lax.axis_index("dp"), lax.axis_index("view"), lax.axis_index("tm")
    core, yh = dp % 2, dp // 2
    x, yl = tm // 2, tm % 2
    sib = dp + 1 - 2 * core
    pair = x * 2 + 1 - yl
    beyond = ((yh - 1 + 2 * yl + n_y) % n_y) * 2 + core

    loads = [
        pltpu.make_async_copy(src, dst, lsem.at[at])
        for at, (src, dst) in enumerate([
            (wq_hbm, w_all.at[tm, pl.ds(0, depth)]), (wo_hbm, w_all.at[tm, pl.ds(depth, depth)]),
            (wk_hbm, w_all.at[tm, pl.ds(lanes, depth)]),
            (wv_hbm, w_all.at[tm, pl.ds(lanes + depth, depth)]),
            (tok_hbm, tok_all.at[tm]), (cot_hbm, cot_all.at[tm]),
        ])
    ]
    for load in loads:
        load.start()

    def copy(src, dst, kind, at, **to):
        return pltpu.make_async_remote_copy(
            src_ref=src, dst_ref=dst, send_sem=ssem.at[kind, at], recv_sem=rsem.at[kind, at],
            device_id=to, device_id_type=MESH,
        )

    barrier = pltpu.get_barrier_semaphore()
    friends = [{"tm": (tm + s) % n_t} for s in range(1, n_t)]
    friends += [{"view": (z + s) % n_z} for s in range(1, n_z)]
    friends += [{"dp": (dp + 2 * s) % n_d} for s in range(1, n_y)]
    friends += [{"view": (z + s) % n_z, "tm": pair} for s in range(1, n_z)]
    friends += [{"dp": sib}, {"dp": beyond, "tm": pair}]
    for friend in friends:
        pl.semaphore_signal(barrier, inc=1, device_id=friend, device_id_type=MESH)
    for load in loads:
        load.wait()
    pl.semaphore_wait(barrier, len(friends))

    def ahead(dx, side):
        return ((x + dx) % n_x) * 2 + side

    def behind(dx, side):
        return ((x - dx + n_x) % n_x) * 2 + side

    def w_half(head, side):
        return w_all.at[head, pl.ds(pl.multiple_of(side * lanes, lanes), lanes)]

    def w_along(dx):
        return copy(w_half(tm, core), w_half(tm, core), KW, dx, tm=ahead(dx, yl))

    def w_across(dx):
        part = w_half(behind(dx, yl), core)
        return copy(part, part, KV, dx, dp=beyond, tm=pair)

    def w_share(dx, side, kind):
        part = w_half(behind(dx, side), core)
        return copy(part, part, kind, dx, dp=sib)

    def w_shared(dx, side, kind):
        part = w_half(behind(dx, side), 1 - core)
        return copy(part, part, kind, dx, dp=sib)

    def tok_pair():
        return copy(tok_all.at[tm], tok_all.at[tm], KT1, 0, tm=pair)

    def tok_along(dx, span, kind):
        return copy(tok_all.at[span], tok_all.at[span], kind, dx, tm=ahead(dx, yl))

    def cot_pair(dx):
        span = behind(dx, yl)
        return copy(cot_all.at[span], cot_all.at[span], KC2, dx, tm=pair)

    def cot_along(dx):
        return copy(cot_all.at[tm], cot_all.at[tm], KC1, dx, tm=ahead(dx, yl))

    x_order = [1, 3, 2] if n_x == 4 else list(range(1, n_x))
    tok_pair().start()
    cot_pair(0).start()
    for dx in x_order:
        w_along(dx).start()

    first = lax.broadcasted_iota(jnp.int32, (rows, lanes), 1) < depth

    def project(head, span, place):
        both = dot_nt(jnp.concatenate([tok_all[span], cot_all[span]], axis=0), w_all[head])
        p_send[place, head, :, :lanes] = jnp.where(
            first, both[:rows, :lanes], both[rows:, :lanes]
        ).astype(BF16)
        p_send[place, head, :, lanes:] = both[:rows, lanes:].astype(BF16)

    def project_own(head):
        project(head, tm, 0)

        @pl.when(head == z)
        def _():
            p_all[z] = p_send[0, head]

        @pl.when(head != z)
        def _():
            copy(p_send.at[0, head], p_all.at[z], KP, (head - z + n_z) % n_z, view=head).start()

    def project_pair(head):
        project(head, pair, 1)
        copy(
            p_send.at[1, head], p_all.at[z], KQ, (head - z + n_z) % n_z, view=head, tm=pair
        ).start()

    project_own(tm)
    for dx in x_order:
        part = w_half(behind(dx, yl), core)
        copy(part, part, KW, dx, tm=ahead(dx, yl)).wait_recv()
        w_share(dx, yl, KS1).start()
    for dx in x_order:
        cot_along(dx).start()
    copy(tok_all.at[pair], tok_all.at[pair], KT1, 0, tm=pair).wait_recv()
    copy(cot_all.at[pair], cot_all.at[pair], KC2, 0, tm=pair).wait_recv()
    project_pair(tm)

    def heads(i, _):
        dx = 1 + (i + z // 2) % (n_x - 1)
        w_shared(dx, yl, KS1).wait_recv()
        project_own(behind(dx, yl))
        project_pair(behind(dx, yl))
        return 0

    if n_x > 1:
        lax.fori_loop(0, n_x - 1, heads, 0)
    for dx in [0] + x_order:
        w_across(dx).start()

    @pl.when(z % 2 == yl)
    def _():
        for d in range(1, n_z):
            cam = (z - d + n_z) % n_z
            copy(p_all.at[cam], p_all.at[cam], KP, d, view=cam).wait_recv()

    @pl.when(z % 2 != yl)
    def _():
        for d in range(n_z):
            cam = (z - d + n_z) % n_z
            copy(p_all.at[cam], p_all.at[cam], KQ, d, view=cam, tm=pair).wait_recv()

    def cot_forward():
        for dx in x_order:
            span = behind(dx, yl)
            copy(cot_all.at[span], cot_all.at[span], KC1, dx, tm=ahead(dx, yl)).wait_recv()
            cot_pair(dx).start()

    total = n_z * rows
    kv_t[...] = p_all[:, :, lanes:].reshape(total, lanes).T
    rig = rig_ref[0]
    factor = depth ** -0.5

    def split(cam):
        qd = p_all[cam, :, :lanes]
        zero = jnp.zeros_like(qd)
        return jnp.where(first, qd, zero), jnp.where(first, zero, qd)

    def attend(step, _):
        cams = [(z + 1 + 2 * step) % n_z, (z + 2 + 2 * step) % n_z]

        @pl.when(step == 0)
        def _():
            cot_forward()
            for dx in x_order:
                tok_along(dx, tm, KT1).start()

        @pl.when(step == 1)
        def _():
            for dx in x_order:
                tok_along(dx, pair, KT2).start()

        query0, grad0 = split(cams[0])
        query1, grad1 = split(cams[1])
        kv = p_all[:, :, lanes:].reshape(total, lanes)
        both = dot_nt(kv, jnp.concatenate([query0, query1, grad0, grad1], axis=0))
        scores = jnp.concatenate(
            [
                jnp.concatenate(
                    [
                        both[b * rows:(b + 1) * rows, q * rows:(q + 1) * rows] * factor
                        + (masks_ref[rig, cams[q], b] - 1).astype(F32) * 1e30
                        for q in range(2)
                    ],
                    axis=1,
                )
                for b in range(n_z)
            ],
            axis=0,
        )
        weights = jnp.exp(scores - jnp.max(scores, axis=0, keepdims=True))
        probs = weights * (1.0 / jnp.sum(weights, axis=0, keepdims=True))
        probs_half = probs.astype(BF16)
        attn = dot(kv_t[depth:], probs_half)
        grad_attn = jnp.concatenate(
            [(query0 + grad0).astype(F32).T[depth:], (query1 + grad1).astype(F32).T[depth:]], axis=1
        )
        delta = jnp.sum(grad_attn * attn.astype(BF16).astype(F32), axis=0, keepdims=True)
        dscore = (probs * (both[:, 2 * rows:] - delta) * factor).astype(BF16)
        dq = dot(kv_t[:depth], dscore)
        out = jnp.concatenate([dq, attn], axis=0)
        for q, cam in enumerate(cams):
            cols = slice(q * rows, (q + 1) * rows)
            x1[cam] = out[:, cols].T.astype(BF16)

            @pl.when(cam == z)
            def _():
                xa1[z] = x1[cam]

            @pl.when(cam != z)
            def _():
                copy(x1.at[cam], xa1.at[z], KX1, (cam - z + n_z) % n_z, view=cam).start()

            pairs[cam, :, :rows] = dscore[:, cols]
            pairs[cam, :, rows:] = probs_half[:, cols]
        return 0

    lax.fori_loop(0, n_z // 2, attend, 0)

    def keys(step, _):
        cams = [(z + 1 + 2 * step) % n_z, (z + 2 + 2 * step) % n_z]
        sums = jnp.zeros((2 * rows, lanes), F32)
        for query in range(n_z):
            block = jnp.concatenate(split(query), axis=0)
            left = jnp.concatenate(
                [pairs[query, pl.ds(pl.multiple_of(cam * rows, rows), rows)] for cam in cams], axis=0
            )
            sums = sums + dot(left, block).astype(BF16).astype(F32)
        for k, cam in enumerate(cams):
            x2[cam] = sums[k * rows:(k + 1) * rows].astype(BF16)

            @pl.when(cam == z)
            def _():
                xa2[z] = x2[cam]

            @pl.when(cam != z)
            def _():
                copy(x2.at[cam], xa2.at[z], KX2, (cam - z + n_z) % n_z, view=cam).start()
        return 0

    lax.fori_loop(0, n_z // 2, keys, 0)

    def hand_on(src, dst, kind, head):
        @pl.when(head == tm)
        def _():
            dst[tm] = src[head]

        @pl.when(head != tm)
        def _():
            copy(src.at[head], dst.at[tm], kind, (head - tm + n_t) % n_t, tm=head).start()

    for dx in [0] + x_order:
        part = w_half(behind(dx, 1 - yl), core)
        copy(part, part, KV, dx, dp=beyond, tm=pair).wait_recv()
        w_share(dx, 1 - yl, KS2).start()

    def arrive1(d, _):
        head = (z - d + n_z) % n_z

        @pl.when(d > 0)
        def _():
            copy(xa1.at[head], xa1.at[head], KX1, d, view=head).wait_recv()

        hand_on(xa1, xb1, KB1, head)
        return 0

    def arrive2(d, _):
        head = (z - d + n_z) % n_z

        @pl.when(d > 0)
        def _():
            copy(xa2.at[head], xa2.at[head], KX2, d, view=head).wait_recv()

        hand_on(xa2, xb2, KB2, head)
        return 0

    lax.fori_loop(0, n_z, lambda i, _: arrive1((i + tm) % n_z, _), 0)
    lax.fori_loop(0, n_z, lambda i, _: arrive2((i + tm) % n_z, _), 0)

    def handed(ref, kind):
        for f in range(1, n_t):
            span = (tm - f + n_t) % n_t
            copy(ref.at[span], ref.at[span], kind, f, tm=span).wait_recv()

    chunk = width // n_z
    keep = pl.multiple_of(core * depth, depth)
    give = pl.multiple_of((1 - core) * depth, depth)

    def core_copy(p):
        return copy(c_send.at[p], c_recv.at[p], KR, p, dp=sib)

    def camera_copy(p, d):
        cam = (z + d) % n_z
        return copy(z_send.at[p, cam], z_recv.at[p, z], KZ, p * n_z + d, view=cam)

    def clip_copy(p, s):
        part = y_recv.at[p, yh]
        return copy(part, part, KY, p * n_y + s, dp=(dp + 2 * s) % n_d)

    def final_copy(p, d):
        part = fin.at[p, core, z]
        return copy(part, part, KF, p * n_z + d, view=(z + d) % n_z)

    def final_share(p, d):
        part = fin.at[p, core, (z - d + n_z) % n_z]
        return copy(part, part, KG, p * n_z + d, dp=sib)

    def core_start(p):
        c_send[p] = g_sum[p, pl.ds(give, depth)].astype(BF16)
        core_copy(p).start()

    def camera_start(p):
        core_copy(p).wait_recv()
        total = (g_sum[p, pl.ds(keep, depth)] + c_recv[p].astype(F32)).astype(BF16)
        for cam in range(n_z):
            z_send[p, cam] = total[:, cam * chunk:(cam + 1) * chunk]
        for d in range(1, n_z):
            camera_copy(p, d).start()

    def clip_start(p):
        total = z_send[p, z].astype(F32)
        for d in range(1, n_z):
            cam = (z - d + n_z) % n_z
            copy(z_recv.at[p, cam], z_recv.at[p, cam], KZ, p * n_z + d, view=cam).wait_recv()
            total = total + z_recv[p, cam].astype(F32)
        y_recv[p, yh] = total.astype(BF16)
        for s in range(1, n_y):
            clip_copy(p, s).start()

    def spread_start(p):
        for s in range(1, n_y):
            other = y_recv.at[p, (yh - s + n_y) % n_y]
            copy(other, other, KY, p * n_y + s, dp=(dp + 2 * s) % n_d).wait_recv()
        total = y_recv[p, 0].astype(F32)
        for s in range(1, n_y):
            total = total + y_recv[p, s].astype(F32)
        fin[p, core, z] = total.astype(BF16)
        for d in range(1, n_z):
            final_copy(p, d).start()
        final_share(p, 0).start()

    def spread_forward(p):
        for d in range(1, n_z):
            part = fin.at[p, core, (z - d + n_z) % n_z]
            copy(part, part, KF, p * n_z + d, view=(z + d) % n_z).wait_recv()
            final_share(p, d).start()

    def spread_end(p):
        for d in range(n_z):
            part = fin.at[p, 1 - core, (z - d + n_z) % n_z]
            copy(part, part, KG, p * n_z + d, dp=sib).wait_recv()
        for side in range(2):
            for cam in range(n_z):
                place = (slice((2 * p + side) * depth, (2 * p + side + 1) * depth),
                         slice(cam * chunk, (cam + 1) * chunk))
                g_ref[place] = fin[p, side, cam]

    def finish(head, sums):
        one, two = xa1[head], xa2[head]
        zero = jnp.zeros_like(one)
        left = jnp.concatenate(
            [
                jnp.concatenate([jnp.where(first, one, zero), two], axis=1),
                jnp.concatenate([jnp.where(first, zero, one), zero], axis=1),
            ],
            axis=0,
        )
        return sums + dot(left, w_all[head])

    for dx in x_order:
        span, other = behind(dx, yl), behind(dx, 1 - yl)
        copy(tok_all.at[span], tok_all.at[span], KT1, dx, tm=ahead(dx, yl)).wait_recv()
        copy(tok_all.at[other], tok_all.at[other], KT2, dx, tm=ahead(dx, yl)).wait_recv()
    for dx in x_order:
        other = behind(dx, 1 - yl)
        copy(cot_all.at[other], cot_all.at[other], KC2, dx, tm=pair).wait_recv()
    tokens = tok_all[...].reshape(n_t * rows, width)
    cots = cot_all[...].reshape(n_t * rows, width)
    handed(xb1, KB1)
    b1 = xb1[...].reshape(n_t * rows, lanes).T
    g_sum[0, :depth] = dot(b1[:depth], tokens)
    g_sum[0, depth:] = dot(b1[depth:], cots)
    core_start(0)
    handed(xb2, KB2)
    g_sum[1] = dot(xb2[...].reshape(n_t * rows, lanes).T, tokens)
    camera_start(0)
    core_start(1)
    camera_start(1)
    for dx in [0] + x_order:
        w_shared(dx, 1 - yl, KS2).wait_recv()
    sums = lax.fori_loop(0, n_z // 2, finish, jnp.zeros((2 * rows, width), F32))
    clip_start(0)
    sums = lax.fori_loop(n_z // 2, n_z, finish, sums)
    both_out[...] = sums.astype(BF16)
    store = pltpu.make_async_copy(both_out, both_hbm, lsem.at[6])
    store.start()
    clip_start(1)
    spread_start(0)
    spread_start(1)
    spread_forward(0)
    spread_end(0)
    spread_forward(1)
    spread_end(1)

    store.wait()
    for dx in [0] + x_order:
        gone = [w_across(dx), w_share(dx, 1 - yl, KS2), cot_pair(dx)]
        if dx:
            gone += [w_along(dx), w_share(dx, yl, KS1), cot_along(dx)]
            gone += [tok_along(dx, tm, KT1), tok_along(dx, pair, KT2)]
        else:
            gone += [tok_pair()]
        for one in gone:
            one.wait_send()
    for step in range(1, n_t):
        head = (tm + step) % n_t
        copy(xa1.at[head], xb1.at[tm], KB1, step, tm=head).wait_send()
        copy(xa2.at[head], xb2.at[tm], KB2, step, tm=head).wait_send()
    for d in range(1, n_z):
        cam = (z + d) % n_z
        copy(x1.at[cam], xa1.at[z], KX1, d, view=cam).wait_send()
        copy(x2.at[cam], xa2.at[z], KX2, d, view=cam).wait_send()
    for dx in range(n_x):
        head = behind(dx, yl)
        d = (head - z + n_z) % n_z
        copy(p_send.at[1, head], p_all.at[z], KQ, d, view=head, tm=pair).wait_send()

        @pl.when(head != z)
        def _():
            copy(p_send.at[0, head], p_all.at[z], KP, d, view=head).wait_send()

    for p in range(2):
        core_copy(p).wait_send()
        for d in range(1, n_z):
            camera_copy(p, d).wait_send()
            final_copy(p, d).wait_send()
        for s in range(1, n_y):
            clip_copy(p, s).wait_send()
        for d in range(n_z):
            final_share(p, d).wait_send()


def shards(n_d, n_z, n_t, tokens, cotangent, w_query, w_key, w_value, w_out, masks, rig_ids):
    rows, width = tokens.shape[2], tokens.shape[3]
    depth = w_query.shape[1]
    lanes = 2 * depth
    vmem = pl.BlockSpec(memory_space=pltpu.VMEM)
    smem = pl.BlockSpec(memory_space=pltpu.SMEM)
    hbm = pl.BlockSpec(memory_space=pltpu.HBM)
    half_block = (n_z, rows, lanes)
    most = 2 * max(n_z, n_t, n_d)
    both, grads = pl.pallas_call(
        functools.partial(kernel, n_d, n_z, n_t, depth),
        out_shape=(
            jax.ShapeDtypeStruct((2 * rows, width), BF16),
            jax.ShapeDtypeStruct((2 * lanes, width), BF16),
        ),
        in_specs=[hbm] * 6 + [smem] * 2,
        out_specs=(hbm, vmem),
        scratch_shapes=[
            pltpu.VMEM((n_t, 2 * lanes, width), BF16),
            pltpu.VMEM((n_t, rows, width), BF16),
            pltpu.VMEM((n_t, rows, width), BF16),
            pltpu.VMEM((2, n_t, rows, 2 * lanes), BF16),
            pltpu.VMEM((n_z, rows, 2 * lanes), BF16),
            pltpu.VMEM((lanes, n_z * rows), BF16),
            pltpu.VMEM((n_z, n_z * rows, 2 * rows), BF16),
            pltpu.VMEM(half_block, BF16),
            pltpu.VMEM(half_block, BF16),
            pltpu.VMEM(half_block, BF16),
            pltpu.VMEM(half_block, BF16),
            pltpu.VMEM((n_t, rows, lanes), BF16),
            pltpu.VMEM((n_t, rows, lanes), BF16),
            pltpu.VMEM((2, lanes, width), F32),
            pltpu.VMEM((2, depth, width), BF16),
            pltpu.VMEM((2, depth, width), BF16),
            pltpu.VMEM((2, n_z, depth, width // n_z), BF16),
            pltpu.VMEM((2, n_z, depth, width // n_z), BF16),
            pltpu.VMEM((2, n_d // 2, depth, width // n_z), BF16),
            pltpu.VMEM((2, 2, n_z, depth, width // n_z), BF16),
            pltpu.VMEM((2 * rows, width), BF16),
            pltpu.SemaphoreType.DMA((7,)),
            pltpu.SemaphoreType.DMA((KINDS, most)),
            pltpu.SemaphoreType.DMA((KINDS, most)),
        ],
        compiler_params=pltpu.CompilerParams(
            collective_id=0, has_side_effects=True, vmem_limit_bytes=60 * 1024 * 1024
        ),
        cost_estimate=pl.CostEstimate(
            flops=3_000_000_000, bytes_accessed=8_000_000, transcendentals=1_000_000
        ),
    )(tokens.reshape(rows, width), cotangent.reshape(rows, width), w_query.T, w_key.T, w_value.T, w_out,
      masks, rig_ids)
    grads = grads.astype(F32)
    return (
        both[rows:].reshape(tokens.shape),
        both[:rows].reshape(tokens.shape),
        grads[:depth].T,
        grads[lanes:lanes + depth].T,
        grads[lanes + depth:].T,
        grads[depth:lanes],
    )


def solution(mesh):
    sizes = mesh.shape
    return jax.shard_map(
        functools.partial(shards, sizes["dp"], sizes["view"], sizes["tm"]),
        mesh=mesh,
        in_specs=(
            P("dp", "view", "tm", None),
            P("dp", "view", "tm", None),
            P(None, "tm"),
            P(None, "tm"),
            P(None, "tm"),
            P("tm", None),
            P(),
            P("dp"),
        ),
        out_specs=(
            P("dp", "view", "tm", None),
            P("dp", "view", "tm", None),
            P(None, "tm"),
            P(None, "tm"),
            P(None, "tm"),
            P("tm", None),
        ),
        check_vma=False,
    )
```

```python
import functools

import jax
import jax.numpy as jnp
from jax import lax
from jax.experimental import pallas as pl
from jax.experimental.pallas import tpu as pltpu
from jax.sharding import PartitionSpec as P

MESH = pl.DeviceIdType.MESH
BF16 = jnp.bfloat16
F32 = jnp.float32

(KW, KV1, KV2, KS1, KS2, KT1, KT2, KC1, KC2, KP, KX1, KX2, KB1, KB2, KR, KZ, KY, KF, KG) = (
    *range(14), 14, 16, 18, 20, 22)
KINDS = 24

NT = (((1,), (1,)), ((), ()))


def dot(a, b):
    return jnp.dot(a, b, preferred_element_type=F32)


def dot_nt(a, b):
    return lax.dot_general(a, b, NT, preferred_element_type=F32)


def receive_places(n_d, n_z, n_t):
    n_x = n_t // 2
    sizes = [n_x] * 9 + [1, n_z, n_z, 1, 1] + [1] * 6 + [n_z] * 2 + [1] * 2
    starts = [(sum(sizes[:k]), sizes[k]) for k in range(KINDS)]
    return starts, sum(sizes)


def kernel(
    n_d, n_z, n_t, depth,
    tok_hbm, cot_hbm, wq_hbm, wk_hbm, wv_hbm, wo_hbm, masks_ref, rig_ref,
    att_hbm, gtok_hbm, g_hbm,
    w_all, tok_all, cot_all, p_send, p_all, kv_t, pairs, x1, x2, xa1, xa2, xb1, xb2,
    g_sum, c_send, c_recv, z_send, z_recv, y_recv, fin, both_out, g_out,
    lsem, ssem, rsem,
):
    rows, width = tok_hbm.shape
    lanes = 2 * depth
    n_x = n_t // 2
    n_y = n_d // 2
    dp, z, tm = lax.axis_index("dp"), lax.axis_index("view"), lax.axis_index("tm")
    core, yh = dp % 2, dp // 2
    x, yl = tm // 2, tm % 2
    sib = dp + 1 - 2 * core
    pair = x * 2 + 1 - yl
    beyond = ((yh - 1 + 2 * yl + n_y) % n_y) * 2 + core

    loads = [
        pltpu.make_async_copy(src, dst, lsem.at[at])
        for at, (src, dst) in enumerate([
            (wq_hbm, w_all.at[tm, pl.ds(0, depth)]), (wo_hbm, w_all.at[tm, pl.ds(depth, depth)]),
            (wk_hbm, w_all.at[tm, pl.ds(lanes, depth)]),
            (wv_hbm, w_all.at[tm, pl.ds(lanes + depth, depth)]),
            (tok_hbm, tok_all.at[tm]), (cot_hbm, cot_all.at[tm]),
        ])
    ]
    for load in loads:
        load.start()

    starts, _ = receive_places(n_d, n_z, n_t)

    def copy(src, dst, kind, at, **to):
        start, size = starts[kind]
        place = start + at if size > 1 else start
        return pltpu.make_async_remote_copy(
            src_ref=src, dst_ref=dst, send_sem=ssem.at[kind], recv_sem=rsem.at[place],
            device_id=to, device_id_type=MESH,
        )

    def arrived(kind, ref):
        copy(ref, ref, kind, 0, dp=sib).wait_recv()

    def gone(kind, ref):
        copy(ref, ref, kind, 0, dp=sib).wait_send()

    def blocks(halves):
        if halves % 2:
            return tok_all.at[0, pl.ds(0, rows // 2)]
        return tok_all.at[pl.ds(0, halves // 2)]

    barrier = pltpu.get_barrier_semaphore()
    friends = [{"tm": (tm + s) % n_t} for s in range(1, n_t)]
    friends += [{"view": (z + s) % n_z} for s in range(1, n_z)]
    friends += [{"dp": (dp + 2 * s) % n_d} for s in range(1, n_y)]
    friends += [{"dp": sib}, {"dp": beyond, "tm": pair}]
    for friend in friends:
        pl.semaphore_signal(barrier, inc=1, device_id=friend, device_id_type=MESH)
    for load in loads:
        load.wait()
    pl.semaphore_wait(barrier, len(friends))

    def ahead(dx, side):
        return ((x + dx) % n_x) * 2 + side

    def behind(dx, side):
        return ((x - dx + n_x) % n_x) * 2 + side

    half, quarter = lanes, depth

    def w_rows(head, start, size):
        return w_all.at[head, pl.ds(pl.multiple_of(start, size), size)]

    def w_mine(head):
        return w_rows(head, core * half, half)

    def w_along(dx):
        return copy(w_mine(tm), w_mine(tm), KW, dx, tm=ahead(dx, yl))

    def w_across(dx):
        head = behind(dx, yl)
        near = w_rows(head, core * half, quarter)
        far = w_rows(head, core * half + quarter, quarter)
        return copy(near, near, KV1, dx, tm=pair), copy(far, far, KV2, dx, dp=beyond, tm=pair)

    def w_share(dx, side, kind):
        part = w_mine(behind(dx, side))
        return copy(part, part, kind, dx, dp=sib)

    def w_shared(dx, side, kind):
        part = w_rows(behind(dx, side), (1 - core) * half, half)
        return copy(part, part, kind, dx, dp=sib)

    x_near = [1, 3] if n_x == 4 else list(range(1, n_x))
    x_far = [2] if n_x == 4 else []
    x_order = x_near + x_far
    for dx in x_near:
        w_along(dx).start()
    for part in w_across(0):
        part.start()

    def tok_pair():
        return copy(tok_all.at[tm], tok_all.at[tm], KT1, 0, tm=pair)

    def tok_along(dx, span, kind):
        return copy(tok_all.at[span], tok_all.at[span], kind, dx, tm=ahead(dx, yl))

    def cot_pair(dx):
        span = behind(dx, yl)
        return copy(cot_all.at[span], cot_all.at[span], KC2, dx, tm=pair)

    def cot_along(dx):
        return copy(cot_all.at[tm], cot_all.at[tm], KC1, dx, tm=ahead(dx, yl))

    first = lax.broadcasted_iota(jnp.int32, (rows, lanes), 1) < depth

    def project(head):
        both = dot_nt(jnp.concatenate([tok_all[tm], cot_all[tm]], axis=0), w_all[head])
        p_send[head, :, :lanes] = jnp.where(first, both[:rows, :lanes], both[rows:, :lanes]).astype(BF16)
        p_send[head, :, lanes:] = both[:rows, lanes:].astype(BF16)

        @pl.when(head == z)
        def _():
            p_all[z] = p_send[head]

        @pl.when(head != z)
        def _():
            copy(p_send.at[head], p_all.at[z], KP, (head - z + n_z) % n_z, view=head).start()

    def w_arrive(dx):
        part = w_mine(behind(dx, yl))
        copy(part, part, KW, dx, tm=ahead(dx, yl)).wait_recv()
        for piece in w_across(dx):
            piece.start()
        w_share(dx, yl, KS1).start()

    def w_arrive_across(dx):
        head = behind(dx, 1 - yl)
        near = w_rows(head, core * half, quarter)
        far = w_rows(head, core * half + quarter, quarter)
        copy(near, near, KV1, dx, tm=pair).wait_recv()
        copy(far, far, KV2, dx, dp=beyond, tm=pair).wait_recv()
        w_share(dx, 1 - yl, KS2).start()

    def project_side(dxs, side, kind):
        def one(i, _):
            dx = dxs[0] + 2 * ((i + z) % len(dxs))
            w_shared(dx, side, kind).wait_recv()
            project(behind(dx, side))
            return 0

        if dxs:
            lax.fori_loop(0, len(dxs), one, 0)

    project(tm)
    w_arrive_across(0)
    for dx in x_near:
        w_arrive(dx)
    for dx in x_far:
        w_along(dx).start()
    project_side([0], 1 - yl, KS2)
    project_side(x_near, yl, KS1)
    for dx in x_near:
        w_arrive_across(dx)
    project_side(x_near, 1 - yl, KS2)
    for dx in x_far:
        w_arrive(dx)
    for dx in x_order:
        cot_along(dx).start()
    project_side(x_far, yl, KS1)
    for dx in x_far:
        w_arrive_across(dx)
    tok_pair().start()
    cot_pair(0).start()
    project_side(x_far, 1 - yl, KS2)

    def cot_forward():
        for dx in x_order:
            span = behind(dx, yl)
            copy(cot_all.at[span], cot_all.at[span], KC1, dx, tm=ahead(dx, yl)).wait_recv()
            cot_pair(dx).start()

    arrived(KP, p_send.at[pl.ds(0, n_z - 1)])

    total = n_z * rows
    kv_t[...] = p_all[:, :, lanes:].reshape(total, lanes).T
    rig = rig_ref[0]
    factor = depth ** -0.5

    def split(cam):
        qd = p_all[cam, :, :lanes]
        zero = jnp.zeros_like(qd)
        return jnp.where(first, qd, zero), jnp.where(first, zero, qd)

    def attend(step, _):
        cams = [(z + 1 + 2 * step) % n_z, (z + 2 + 2 * step) % n_z]

        @pl.when(step == 0)
        def _():
            cot_forward()
            for dx in x_order:
                tok_along(dx, tm, KT1).start()

        @pl.when(step == 1)
        def _():
            copy(tok_all.at[pair], tok_all.at[pair], KT1, 0, tm=pair).wait_recv()
            for dx in x_order:
                tok_along(dx, pair, KT2).start()

        query0, grad0 = split(cams[0])
        query1, grad1 = split(cams[1])
        kv = p_all[:, :, lanes:].reshape(total, lanes)
        both = dot_nt(kv, jnp.concatenate([query0, query1, grad0, grad1], axis=0))
        scores = jnp.concatenate(
            [
                jnp.concatenate(
                    [
                        both[b * rows:(b + 1) * rows, q * rows:(q + 1) * rows] * factor
                        + (masks_ref[rig, cams[q], b] - 1).astype(F32) * 1e30
                        for q in range(2)
                    ],
                    axis=1,
                )
                for b in range(n_z)
            ],
            axis=0,
        )
        weights = jnp.exp(scores - jnp.max(scores, axis=0, keepdims=True))
        probs = weights * (1.0 / jnp.sum(weights, axis=0, keepdims=True))
        probs_half = probs.astype(BF16)
        attn = dot(kv_t[depth:], probs_half)
        grad_attn = jnp.concatenate(
            [(query0 + grad0).astype(F32).T[depth:], (query1 + grad1).astype(F32).T[depth:]], axis=1
        )
        delta = jnp.sum(grad_attn * attn.astype(BF16).astype(F32), axis=0, keepdims=True)
        dscore = (probs * (both[:, 2 * rows:] - delta) * factor).astype(BF16)
        dq = dot(kv_t[:depth], dscore)
        out = jnp.concatenate([dq, attn], axis=0)
        for q, cam in enumerate(cams):
            cols = slice(q * rows, (q + 1) * rows)
            x1[cam] = out[:, cols].T.astype(BF16)

            @pl.when(cam == z)
            def _():
                xa1[z] = x1[cam]

            @pl.when(cam != z)
            def _():
                copy(x1.at[cam], xa1.at[z], KX1, (cam - z + n_z) % n_z, view=cam).start()

            pairs[cam, :, :rows] = dscore[:, cols]
            pairs[cam, :, rows:] = probs_half[:, cols]
        return 0

    lax.fori_loop(0, n_z // 2, attend, 0)

    def keys(step, _):
        cams = [(z + 1 + 2 * step) % n_z, (z + 2 + 2 * step) % n_z]
        sums = jnp.zeros((2 * rows, lanes), F32)
        for query in range(n_z):
            block = jnp.concatenate(split(query), axis=0)
            left = jnp.concatenate(
                [pairs[query, pl.ds(pl.multiple_of(cam * rows, rows), rows)] for cam in cams], axis=0
            )
            sums = sums + dot(left, block).astype(BF16).astype(F32)
        for k, cam in enumerate(cams):
            x2[cam] = sums[k * rows:(k + 1) * rows].astype(BF16)

            @pl.when(cam == z)
            def _():
                xa2[z] = x2[cam]

            @pl.when(cam != z)
            def _():
                copy(x2.at[cam], xa2.at[z], KX2, (cam - z + n_z) % n_z, view=cam).start()
        return 0

    lax.fori_loop(0, n_z // 2, keys, 0)

    def hand_on(src, dst, kind, head):
        @pl.when(head == tm)
        def _():
            dst[tm] = src[head]

        @pl.when(head != tm)
        def _():
            copy(src.at[head], dst.at[tm], kind, (head - tm + n_t) % n_t, tm=head).start()

    def arrive1(d, _):
        head = (z - d + n_z) % n_z

        @pl.when(d > 0)
        def _():
            copy(xa1.at[head], xa1.at[head], KX1, d, view=head).wait_recv()

        hand_on(xa1, xb1, KB1, head)
        return 0

    def arrive2(d, _):
        head = (z - d + n_z) % n_z

        @pl.when(d > 0)
        def _():
            copy(xa2.at[head], xa2.at[head], KX2, d, view=head).wait_recv()

        hand_on(xa2, xb2, KB2, head)
        return 0

    lax.fori_loop(0, n_z, lambda i, _: arrive1((i + tm) % n_z, _), 0)
    lax.fori_loop(0, n_z, lambda i, _: arrive2((i + tm) % n_z, _), 0)

    chunk = width // n_z
    keep = pl.multiple_of(core * depth, depth)
    give = pl.multiple_of((1 - core) * depth, depth)

    def core_copy(p):
        return copy(c_send.at[p], c_recv.at[p], KR + p, 0, dp=sib)

    def camera_copy(p, d):
        cam = (z + d) % n_z
        return copy(z_send.at[p, cam], z_recv.at[p, z], KZ + p, d, view=cam)

    def clip_copy(p, s):
        part = y_recv.at[p, yh]
        return copy(part, part, KY + p, s, dp=(dp + 2 * s) % n_d)

    def final_copy(p, d):
        part = fin.at[p, core, z]
        return copy(part, part, KF + p, d, view=(z + d) % n_z)

    def final_share(p, d):
        part = fin.at[p, core, (z - d + n_z) % n_z]
        return copy(part, part, KG + p, d, dp=sib)

    def core_start(p):
        c_send[p] = g_sum[p, pl.ds(give, depth)].astype(BF16)
        core_copy(p).start()

    def camera_start(p):
        core_copy(p).wait_recv()
        total = (g_sum[p, pl.ds(keep, depth)] + c_recv[p].astype(F32)).astype(BF16)
        for cam in range(n_z):
            z_send[p, cam] = total[:, cam * chunk:(cam + 1) * chunk]
        for d in range(1, n_z):
            camera_copy(p, d).start()

    def clip_start(p):
        total = z_send[p, z].astype(F32)
        arrived(KZ + p, z_recv.at[p, pl.ds(0, n_z - 1)])
        for d in range(1, n_z):
            total = total + z_recv[p, (z - d + n_z) % n_z].astype(F32)
        y_recv[p, yh] = total.astype(BF16)
        for s in range(1, n_y):
            clip_copy(p, s).start()

    def spread_start(p):
        if n_y > 1:
            arrived(KY + p, y_recv.at[p, pl.ds(0, n_y - 1)])
        total = y_recv[p, 0].astype(F32)
        for s in range(1, n_y):
            total = total + y_recv[p, s].astype(F32)
        fin[p, core, z] = total.astype(BF16)
        for d in range(1, n_z):
            final_copy(p, d).start()
        final_share(p, 0).start()

    def spread_forward(p):
        for d in range(1, n_z):
            part = fin.at[p, core, (z - d + n_z) % n_z]
            copy(part, part, KF + p, d, view=(z + d) % n_z).wait_recv()
            final_share(p, d).start()

    def spread_end(p):
        arrived(KG + p, fin.at[p, 1 - core])
        for side in range(2):
            for cam in range(n_z):
                place = (slice((2 * p + side) * depth, (2 * p + side + 1) * depth),
                         slice(cam * chunk, (cam + 1) * chunk))
                g_out[place] = fin[p, side, cam].astype(F32)
        return g_store(p)

    def g_store(p):
        part = pl.ds(p * lanes, lanes)
        return pltpu.make_async_copy(g_out.at[part], g_hbm.at[part], lsem.at[8 + p])

    def finish(head, sums):
        one, two = xa1[head], xa2[head]
        zero = jnp.zeros_like(one)
        left = jnp.concatenate(
            [
                jnp.concatenate([jnp.where(first, one, zero), two], axis=1),
                jnp.concatenate([jnp.where(first, zero, one), zero], axis=1),
            ],
            axis=0,
        )
        return sums + dot(left, w_all[head])

    for dx in x_order:
        span, other = behind(dx, yl), behind(dx, 1 - yl)
        copy(tok_all.at[span], tok_all.at[span], KT1, dx, tm=ahead(dx, yl)).wait_recv()
        copy(tok_all.at[other], tok_all.at[other], KT2, dx, tm=ahead(dx, yl)).wait_recv()
    for dx in [0] + x_order:
        other = behind(dx, 1 - yl)
        copy(cot_all.at[other], cot_all.at[other], KC2, dx, tm=pair).wait_recv()
    tokens = tok_all[...].reshape(n_t * rows, width)
    cots = cot_all[...].reshape(n_t * rows, width)
    arrived(KB1, xb1.at[pl.ds(0, n_t - 1)])
    b1 = xb1[...].reshape(n_t * rows, lanes).T
    g_sum[0, :depth] = dot(b1[:depth], tokens)
    g_sum[0, depth:] = dot(b1[depth:], cots)
    core_start(0)
    arrived(KB2, xb2.at[pl.ds(0, n_t - 1)])
    g_sum[1] = dot(xb2[...].reshape(n_t * rows, lanes).T, tokens)
    camera_start(0)
    core_start(1)
    camera_start(1)
    sums = lax.fori_loop(0, n_z // 2, finish, jnp.zeros((2 * rows, width), F32))
    clip_start(0)
    sums = lax.fori_loop(n_z // 2, n_z, finish, sums)
    both_out[...] = sums.astype(BF16)
    stores = [
        pltpu.make_async_copy(both_out.at[pl.ds(0, rows)], gtok_hbm, lsem.at[6]),
        pltpu.make_async_copy(both_out.at[pl.ds(rows, rows)], att_hbm, lsem.at[7]),
    ]
    for store in stores:
        store.start()
    clip_start(1)
    spread_start(0)
    spread_start(1)
    spread_forward(0)
    stores.append(spread_end(0))
    stores[-1].start()
    spread_forward(1)
    stores.append(spread_end(1))
    stores[-1].start()

    far_units = n_x - 1
    gone(KV1, blocks(n_x))
    gone(KV2, blocks(n_x))
    gone(KS2, blocks(2 * n_x))
    gone(KC2, blocks(2 * n_x))
    gone(KT1, blocks(2 * n_x))
    if far_units:
        for kind in (KW, KS1, KT2, KC1):
            gone(kind, blocks(2 * far_units))
    gone(KP, p_send.at[pl.ds(0, n_z - 1)])
    gone(KX1, x1.at[pl.ds(0, n_z - 1)])
    gone(KX2, x2.at[pl.ds(0, n_z - 1)])
    gone(KB1, xb1.at[pl.ds(0, n_t - 1)])
    gone(KB2, xb2.at[pl.ds(0, n_t - 1)])
    for p in range(2):
        gone(KR + p, c_send.at[p])
        gone(KZ + p, z_send.at[p, pl.ds(0, n_z - 1)])
        if n_y > 1:
            gone(KY + p, y_recv.at[p, pl.ds(0, n_y - 1)])
        gone(KF + p, fin.at[p, 0, pl.ds(0, n_z - 1)])
        gone(KG + p, fin.at[p, 0])
    for store in stores:
        store.wait()


def shards(n_d, n_z, n_t, tokens, cotangent, w_query, w_key, w_value, w_out, masks, rig_ids):
    rows, width = tokens.shape[2], tokens.shape[3]
    depth = w_query.shape[1]
    lanes = 2 * depth
    smem = pl.BlockSpec(memory_space=pltpu.SMEM)
    hbm = pl.BlockSpec(memory_space=pltpu.HBM)
    half_block = (n_z, rows, lanes)
    _, places = receive_places(n_d, n_z, n_t)
    attended, grad_rows, grads = pl.pallas_call(
        functools.partial(kernel, n_d, n_z, n_t, depth),
        out_shape=(
            jax.ShapeDtypeStruct((rows, width), BF16),
            jax.ShapeDtypeStruct((rows, width), BF16),
            jax.ShapeDtypeStruct((2 * lanes, width), F32),
        ),
        in_specs=[hbm] * 6 + [smem] * 2,
        out_specs=(hbm, hbm, hbm),
        scratch_shapes=[
            pltpu.VMEM((n_t, 2 * lanes, width), BF16),
            pltpu.VMEM((n_t, rows, width), BF16),
            pltpu.VMEM((n_t, rows, width), BF16),
            pltpu.VMEM((n_z, rows, 2 * lanes), BF16),
            pltpu.VMEM((n_z, rows, 2 * lanes), BF16),
            pltpu.VMEM((lanes, n_z * rows), BF16),
            pltpu.VMEM((n_z, n_z * rows, 2 * rows), BF16),
            pltpu.VMEM(half_block, BF16),
            pltpu.VMEM(half_block, BF16),
            pltpu.VMEM(half_block, BF16),
            pltpu.VMEM(half_block, BF16),
            pltpu.VMEM((n_t, rows, lanes), BF16),
            pltpu.VMEM((n_t, rows, lanes), BF16),
            pltpu.VMEM((2, lanes, width), F32),
            pltpu.VMEM((2, depth, width), BF16),
            pltpu.VMEM((2, depth, width), BF16),
            pltpu.VMEM((2, n_z, depth, width // n_z), BF16),
            pltpu.VMEM((2, n_z, depth, width // n_z), BF16),
            pltpu.VMEM((2, n_d // 2, depth, width // n_z), BF16),
            pltpu.VMEM((2, 2, n_z, depth, width // n_z), BF16),
            pltpu.VMEM((2 * rows, width), BF16),
            pltpu.VMEM((2 * lanes, width), F32),
            pltpu.SemaphoreType.DMA((10,)),
            pltpu.SemaphoreType.DMA((KINDS,)),
            pltpu.SemaphoreType.DMA((places,)),
        ],
        compiler_params=pltpu.CompilerParams(
            collective_id=0, has_side_effects=True, vmem_limit_bytes=60 * 1024 * 1024
        ),
        cost_estimate=pl.CostEstimate(
            flops=3_000_000_000, bytes_accessed=8_000_000, transcendentals=1_000_000
        ),
    )(tokens.reshape(rows, width), cotangent.reshape(rows, width), w_query.T, w_key.T, w_value.T, w_out,
      masks, rig_ids)
    return (
        attended.reshape(tokens.shape),
        grad_rows.reshape(tokens.shape),
        grads[:depth].T,
        grads[lanes:lanes + depth].T,
        grads[lanes + depth:].T,
        grads[depth:lanes],
    )


def solution(mesh):
    sizes = mesh.shape
    return jax.shard_map(
        functools.partial(shards, sizes["dp"], sizes["view"], sizes["tm"]),
        mesh=mesh,
        in_specs=(
            P("dp", "view", "tm", None),
            P("dp", "view", "tm", None),
            P(None, "tm"),
            P(None, "tm"),
            P(None, "tm"),
            P("tm", None),
            P(),
            P("dp"),
        ),
        out_specs=(
            P("dp", "view", "tm", None),
            P("dp", "view", "tm", None),
            P(None, "tm"),
            P(None, "tm"),
            P(None, "tm"),
            P("tm", None),
        ),
        check_vma=False,
    )
```

```python
import functools

import jax
import jax.numpy as jnp
from jax import lax
from jax.experimental import pallas as pl
from jax.experimental.pallas import tpu as pltpu
from jax.sharding import PartitionSpec as P

MESH = pl.DeviceIdType.MESH
BF16 = jnp.bfloat16
F32 = jnp.float32

(KW, KV1, KV2, KS1, KS2, KT1, KT2, KC1, KC2, KP, KX1, KX2, KB1, KB2, KR, KZ, KY, KF, KG,
 KW2, KC3, KT3, KT4) = (*range(14), 14, 16, 18, 20, 22, *range(24, 28))
KINDS = 28

NT = (((1,), (1,)), ((), ()))


def dot(a, b):
    return jnp.dot(a, b, preferred_element_type=F32)


def dot_nt(a, b):
    return lax.dot_general(a, b, NT, preferred_element_type=F32)


def receive_places(n_d, n_z, n_t):
    n_x = n_t // 2
    sizes = [n_x] * 9 + [1, n_z, n_z, 1, 1] + [1] * 6 + [n_z] * 2 + [1] * 2 + [2] * 4
    starts = [(sum(sizes[:k]), sizes[k]) for k in range(KINDS)]
    return starts, sum(sizes)


def kernel(
    n_d, n_z, n_t, depth,
    tok_hbm, cot_hbm, wq_hbm, wk_hbm, wv_hbm, wo_hbm, masks_ref, rig_ref,
    att_hbm, gtok_hbm, g_hbm,
    w_all, tok_all, cot_all, p_send, p_all, kv_t, pairs, x1, x2, xa1, xa2, xb1, xb2,
    g_sum, c_send, c_recv, z_send, z_recv, y_recv, fin, both_out, g_out,
    lsem, ssem, rsem,
):
    rows, width = tok_hbm.shape
    lanes = 2 * depth
    n_x = n_t // 2
    n_y = n_d // 2
    dp, z, tm = lax.axis_index("dp"), lax.axis_index("view"), lax.axis_index("tm")
    core, yh = dp % 2, dp // 2
    x, yl = tm // 2, tm % 2
    sib = dp + 1 - 2 * core
    pair = x * 2 + 1 - yl
    beyond = ((yh - 1 + 2 * yl + n_y) % n_y) * 2 + core

    loads = [
        pltpu.make_async_copy(src, dst, lsem.at[at])
        for at, (src, dst) in enumerate([
            (wq_hbm, w_all.at[tm, pl.ds(0, depth)]), (wo_hbm, w_all.at[tm, pl.ds(depth, depth)]),
            (wk_hbm, w_all.at[tm, pl.ds(lanes, depth)]),
            (wv_hbm, w_all.at[tm, pl.ds(lanes + depth, depth)]),
            (tok_hbm, tok_all.at[tm]), (cot_hbm, cot_all.at[tm]),
        ])
    ]
    for load in loads:
        load.start()

    starts, _ = receive_places(n_d, n_z, n_t)

    def copy(src, dst, kind, at, **to):
        start, size = starts[kind]
        place = start + at if size > 1 else start
        return pltpu.make_async_remote_copy(
            src_ref=src, dst_ref=dst, send_sem=ssem.at[kind], recv_sem=rsem.at[place],
            device_id=to, device_id_type=MESH,
        )

    def arrived(kind, ref):
        copy(ref, ref, kind, 0, dp=sib).wait_recv()

    def gone(kind, ref):
        copy(ref, ref, kind, 0, dp=sib).wait_send()

    def blocks(halves):
        if halves % 2:
            return tok_all.at[0, pl.ds(0, rows // 2)]
        return tok_all.at[pl.ds(0, halves // 2)]

    barrier = pltpu.get_barrier_semaphore()
    friends = [{"tm": (tm + s) % n_t} for s in range(1, n_t)]
    friends += [{"view": (z + s) % n_z} for s in range(1, n_z)]
    friends += [{"dp": (dp + 2 * s) % n_d} for s in range(1, n_y)]
    friends += [{"dp": sib}, {"dp": beyond, "tm": pair}]
    for friend in friends:
        pl.semaphore_signal(barrier, inc=1, device_id=friend, device_id_type=MESH)
    for load in loads:
        load.wait()
    pl.semaphore_wait(barrier, len(friends))

    def ahead(dx, side):
        return ((x + dx) % n_x) * 2 + side

    def behind(dx, side):
        return ((x - dx + n_x) % n_x) * 2 + side

    half, quarter = lanes, depth

    def w_rows(head, start, size):
        return w_all.at[head, pl.ds(pl.multiple_of(start, size), size)]

    def w_mine(head):
        return w_rows(head, core * half, half)

    def w_along(dx):
        return copy(w_mine(tm), w_mine(tm), KW, dx, tm=ahead(dx, yl))

    def w_across(dx):
        head = behind(dx, yl)
        near = w_rows(head, core * half, quarter)
        far = w_rows(head, core * half + quarter, quarter)
        return copy(near, near, KV1, dx, tm=pair), copy(far, far, KV2, dx, dp=beyond, tm=pair)

    def w_share(dx, side, kind):
        part = w_mine(behind(dx, side))
        return copy(part, part, kind, dx, dp=sib)

    def w_shared(dx, side, kind):
        part = w_rows(behind(dx, side), (1 - core) * half, half)
        return copy(part, part, kind, dx, dp=sib)

    relays = [(1, 1), (3, 0)]

    def relay(ref, kind, side):
        if not x_far:
            return
        for dx, part in relays:
            rows_part = ref.at[behind(dx, side), pl.ds(part * (rows // 2), rows // 2)]
            copy(rows_part, rows_part, kind, part, tm=ahead(dx, yl)).start()

    def relayed(ref, kind, side):
        for dx in x_far:
            for part in range(2):
                rows_part = ref.at[behind(dx, side), pl.ds(part * (rows // 2), rows // 2)]
                copy(rows_part, rows_part, kind, part, tm=pair).wait_recv()

    def w_piece(dx, part):
        return w_rows(behind(dx, yl), core * half + part * quarter, quarter)

    x_near = [1, 3] if n_x == 4 else list(range(1, n_x))
    x_far = [2] if n_x == 4 else []
    x_order = x_near + x_far
    for dx in x_near:
        w_along(dx).start()
    for part in w_across(0):
        part.start()

    def tok_pair():
        return copy(tok_all.at[tm], tok_all.at[tm], KT1, 0, tm=pair)

    def tok_along(dx, span, kind):
        return copy(tok_all.at[span], tok_all.at[span], kind, dx, tm=ahead(dx, yl))

    def cot_pair(dx):
        span = behind(dx, yl)
        return copy(cot_all.at[span], cot_all.at[span], KC2, dx, tm=pair)

    def cot_along(dx):
        return copy(cot_all.at[tm], cot_all.at[tm], KC1, dx, tm=ahead(dx, yl))

    first = lax.broadcasted_iota(jnp.int32, (rows, lanes), 1) < depth

    def project(head):
        both = dot_nt(jnp.concatenate([tok_all[tm], cot_all[tm]], axis=0), w_all[head])
        p_send[head, :, :lanes] = jnp.where(first, both[:rows, :lanes], both[rows:, :lanes]).astype(BF16)
        p_send[head, :, lanes:] = both[:rows, lanes:].astype(BF16)

        @pl.when(head == z)
        def _():
            p_all[z] = p_send[head]

        @pl.when(head != z)
        def _():
            copy(p_send.at[head], p_all.at[z], KP, (head - z + n_z) % n_z, view=head).start()

    def w_arrive(dx):
        if dx in x_far:
            for part in range(2):
                piece = w_piece(dx, part)
                copy(piece, piece, KW2, part, tm=pair).wait_recv()
        else:
            block = w_mine(behind(dx, yl))
            copy(block, block, KW, dx, tm=ahead(dx, yl)).wait_recv()
            if x_far:
                part = dict(relays)[dx]
                piece = w_piece(dx, part)
                copy(piece, piece, KW2, part, tm=ahead(dx, yl)).start()
        for piece in w_across(dx):
            piece.start()
        w_share(dx, yl, KS1).start()

    def w_arrive_across(dx):
        head = behind(dx, 1 - yl)
        near = w_rows(head, core * half, quarter)
        far = w_rows(head, core * half + quarter, quarter)
        copy(near, near, KV1, dx, tm=pair).wait_recv()
        copy(far, far, KV2, dx, dp=beyond, tm=pair).wait_recv()
        w_share(dx, 1 - yl, KS2).start()

    def project_side(dxs, side, kind):
        def one(i, _):
            dx = dxs[0] + 2 * ((i + z) % len(dxs))
            w_shared(dx, side, kind).wait_recv()
            project(behind(dx, side))
            return 0

        if dxs:
            lax.fori_loop(0, len(dxs), one, 0)

    tok_pair().start()
    project(tm)
    w_arrive_across(0)
    for dx in x_near:
        w_arrive(dx)
    project_side([0], 1 - yl, KS2)
    project_side(x_near, yl, KS1)
    for dx in x_far:
        w_arrive(dx)
    for dx in x_near:
        w_arrive_across(dx)
    for dx in x_near:
        cot_along(dx).start()
        tok_along(dx, tm, KT1).start()
    project_side(x_near, 1 - yl, KS2)
    project_side(x_far, yl, KS1)
    for dx in x_far:
        w_arrive_across(dx)
    cot_pair(0).start()
    project_side(x_far, 1 - yl, KS2)

    for dx in x_near:
        span = behind(dx, yl)
        copy(cot_all.at[span], cot_all.at[span], KC1, dx, tm=pair).wait_recv()
        cot_pair(dx).start()
    relay(cot_all, KC3, yl)
    for dx in x_near:
        span = behind(dx, yl)
        copy(tok_all.at[span], tok_all.at[span], KT1, dx, tm=pair).wait_recv()
    relay(tok_all, KT3, yl)
    copy(tok_all.at[pair], tok_all.at[pair], KT1, 0, tm=pair).wait_recv()
    for dx in x_near:
        tok_along(dx, pair, KT2).start()

    arrived(KP, p_send.at[pl.ds(0, n_z - 1)])

    total = n_z * rows
    kv_t[...] = p_all[:, :, lanes:].reshape(total, lanes).T
    rig = rig_ref[0]
    factor = depth ** -0.5

    def split(cam):
        qd = p_all[cam, :, :lanes]
        zero = jnp.zeros_like(qd)
        return jnp.where(first, qd, zero), jnp.where(first, zero, qd)

    def attend(step, _):
        cams = [(z + 1 + 2 * step) % n_z, (z + 2 + 2 * step) % n_z]

        @pl.when(step == 0)
        def _():
            relayed(cot_all, KC3, yl)
            for dx in x_far:
                cot_pair(dx).start()

        @pl.when(step == 1)
        def _():
            for dx in x_near:
                span = behind(dx, 1 - yl)
                copy(tok_all.at[span], tok_all.at[span], KT2, dx, tm=pair).wait_recv()
            relay(tok_all, KT4, 1 - yl)

        query0, grad0 = split(cams[0])
        query1, grad1 = split(cams[1])
        kv = p_all[:, :, lanes:].reshape(total, lanes)
        both = dot_nt(kv, jnp.concatenate([query0, query1, grad0, grad1], axis=0))
        scores = jnp.concatenate(
            [
                jnp.concatenate(
                    [
                        both[b * rows:(b + 1) * rows, q * rows:(q + 1) * rows] * factor
                        + (masks_ref[rig, cams[q], b] - 1).astype(F32) * 1e30
                        for q in range(2)
                    ],
                    axis=1,
                )
                for b in range(n_z)
            ],
            axis=0,
        )
        weights = jnp.exp(scores - jnp.max(scores, axis=0, keepdims=True))
        probs = weights * (1.0 / jnp.sum(weights, axis=0, keepdims=True))
        probs_half = probs.astype(BF16)
        attn = dot(kv_t[depth:], probs_half)
        grad_attn = jnp.concatenate(
            [(query0 + grad0).astype(F32).T[depth:], (query1 + grad1).astype(F32).T[depth:]], axis=1
        )
        delta = jnp.sum(grad_attn * attn.astype(BF16).astype(F32), axis=0, keepdims=True)
        dscore = (probs * (both[:, 2 * rows:] - delta) * factor).astype(BF16)
        dq = dot(kv_t[:depth], dscore)
        out = jnp.concatenate([dq, attn], axis=0)
        for q, cam in enumerate(cams):
            cols = slice(q * rows, (q + 1) * rows)
            x1[cam] = out[:, cols].T.astype(BF16)

            @pl.when(cam == z)
            def _():
                xa1[z] = x1[cam]

            @pl.when(cam != z)
            def _():
                copy(x1.at[cam], xa1.at[z], KX1, (cam - z + n_z) % n_z, view=cam).start()

            pairs[cam, :, :rows] = dscore[:, cols]
            pairs[cam, :, rows:] = probs_half[:, cols]
        return 0

    lax.fori_loop(0, n_z // 2, attend, 0)

    def keys(step, _):
        cams = [(z + 1 + 2 * step) % n_z, (z + 2 + 2 * step) % n_z]
        sums = jnp.zeros((2 * rows, lanes), F32)
        for query in range(n_z):
            block = jnp.concatenate(split(query), axis=0)
            left = jnp.concatenate(
                [pairs[query, pl.ds(pl.multiple_of(cam * rows, rows), rows)] for cam in cams], axis=0
            )
            sums = sums + dot(left, block).astype(BF16).astype(F32)
        for k, cam in enumerate(cams):
            x2[cam] = sums[k * rows:(k + 1) * rows].astype(BF16)

            @pl.when(cam == z)
            def _():
                xa2[z] = x2[cam]

            @pl.when(cam != z)
            def _():
                copy(x2.at[cam], xa2.at[z], KX2, (cam - z + n_z) % n_z, view=cam).start()
        return 0

    lax.fori_loop(0, n_z // 2, keys, 0)

    def hand_on(src, dst, kind, head):
        @pl.when(head == tm)
        def _():
            dst[tm] = src[head]

        @pl.when(head != tm)
        def _():
            copy(src.at[head], dst.at[tm], kind, (head - tm + n_t) % n_t, tm=head).start()

    def arrive1(d, _):
        head = (z - d + n_z) % n_z

        @pl.when(d > 0)
        def _():
            copy(xa1.at[head], xa1.at[head], KX1, d, view=head).wait_recv()

        hand_on(xa1, xb1, KB1, head)
        return 0

    def arrive2(d, _):
        head = (z - d + n_z) % n_z

        @pl.when(d > 0)
        def _():
            copy(xa2.at[head], xa2.at[head], KX2, d, view=head).wait_recv()

        hand_on(xa2, xb2, KB2, head)
        return 0

    lax.fori_loop(0, n_z, lambda i, _: arrive1((i + tm) % n_z, _), 0)
    lax.fori_loop(0, n_z, lambda i, _: arrive2((i + tm) % n_z, _), 0)

    chunk = width // n_z
    keep = pl.multiple_of(core * depth, depth)
    give = pl.multiple_of((1 - core) * depth, depth)

    def core_copy(p):
        return copy(c_send.at[p], c_recv.at[p], KR + p, 0, dp=sib)

    def camera_copy(p, d):
        cam = (z + d) % n_z
        return copy(z_send.at[p, cam], z_recv.at[p, z], KZ + p, d, view=cam)

    def clip_copy(p, s):
        part = y_recv.at[p, yh]
        return copy(part, part, KY + p, s, dp=(dp + 2 * s) % n_d)

    def final_copy(p, d):
        part = fin.at[p, core, z]
        return copy(part, part, KF + p, d, view=(z + d) % n_z)

    def final_share(p, d):
        part = fin.at[p, core, (z - d + n_z) % n_z]
        return copy(part, part, KG + p, d, dp=sib)

    def core_start(p):
        c_send[p] = g_sum[p, pl.ds(give, depth)].astype(BF16)
        core_copy(p).start()

    def camera_start(p):
        core_copy(p).wait_recv()
        total = (g_sum[p, pl.ds(keep, depth)] + c_recv[p].astype(F32)).astype(BF16)
        for cam in range(n_z):
            z_send[p, cam] = total[:, cam * chunk:(cam + 1) * chunk]
        for d in range(1, n_z):
            camera_copy(p, d).start()

    def clip_start(p):
        total = z_send[p, z].astype(F32)
        arrived(KZ + p, z_recv.at[p, pl.ds(0, n_z - 1)])
        for d in range(1, n_z):
            total = total + z_recv[p, (z - d + n_z) % n_z].astype(F32)
        y_recv[p, yh] = total.astype(BF16)
        for s in range(1, n_y):
            clip_copy(p, s).start()

    def spread_start(p):
        if n_y > 1:
            arrived(KY + p, y_recv.at[p, pl.ds(0, n_y - 1)])
        total = y_recv[p, 0].astype(F32)
        for s in range(1, n_y):
            total = total + y_recv[p, s].astype(F32)
        fin[p, core, z] = total.astype(BF16)
        for d in range(1, n_z):
            final_copy(p, d).start()
        final_share(p, 0).start()

    def spread_forward(p):
        for d in range(1, n_z):
            part = fin.at[p, core, (z - d + n_z) % n_z]
            copy(part, part, KF + p, d, view=(z + d) % n_z).wait_recv()
            final_share(p, d).start()

    def spread_end(p):
        arrived(KG + p, fin.at[p, 1 - core])
        for side in range(2):
            for cam in range(n_z):
                place = (slice((2 * p + side) * depth, (2 * p + side + 1) * depth),
                         slice(cam * chunk, (cam + 1) * chunk))
                g_out[place] = fin[p, side, cam]
        return g_store(p)

    def g_store(p):
        part = pl.ds(p * lanes, lanes)
        return pltpu.make_async_copy(g_out.at[part], g_hbm.at[part], lsem.at[8 + p])

    def finish(head, sums):
        one, two = xa1[head], xa2[head]
        zero = jnp.zeros_like(one)
        left = jnp.concatenate(
            [
                jnp.concatenate([jnp.where(first, one, zero), two], axis=1),
                jnp.concatenate([jnp.where(first, zero, one), zero], axis=1),
            ],
            axis=0,
        )
        return sums + dot(left, w_all[head])

    relayed(tok_all, KT3, yl)
    relayed(tok_all, KT4, 1 - yl)
    for dx in [0] + x_order:
        other = behind(dx, 1 - yl)
        copy(cot_all.at[other], cot_all.at[other], KC2, dx, tm=pair).wait_recv()
    tokens = tok_all[...].reshape(n_t * rows, width)
    cots = cot_all[...].reshape(n_t * rows, width)
    arrived(KB1, xb1.at[pl.ds(0, n_t - 1)])
    b1 = xb1[...].reshape(n_t * rows, lanes).T
    g_sum[0, :depth] = dot(b1[:depth], tokens)
    g_sum[0, depth:] = dot(b1[depth:], cots)
    core_start(0)
    arrived(KB2, xb2.at[pl.ds(0, n_t - 1)])
    g_sum[1] = dot(xb2[...].reshape(n_t * rows, lanes).T, tokens)
    camera_start(0)
    core_start(1)
    camera_start(1)
    sums = lax.fori_loop(0, n_z // 2, finish, jnp.zeros((2 * rows, width), F32))
    clip_start(0)
    sums = lax.fori_loop(n_z // 2, n_z, finish, sums)
    both_out[...] = sums.astype(BF16)
    stores = [
        pltpu.make_async_copy(both_out.at[pl.ds(0, rows)], gtok_hbm, lsem.at[6]),
        pltpu.make_async_copy(both_out.at[pl.ds(rows, rows)], att_hbm, lsem.at[7]),
    ]
    for store in stores:
        store.start()
    clip_start(1)
    spread_start(0)
    spread_start(1)
    spread_forward(0)
    stores.append(spread_end(0))
    stores[-1].start()
    spread_forward(1)
    stores.append(spread_end(1))
    stores[-1].start()

    near = len(x_near)
    gone(KV1, blocks(n_x))
    gone(KV2, blocks(n_x))
    gone(KS2, blocks(2 * n_x))
    gone(KC2, blocks(2 * n_x))
    gone(KT1, blocks(2 * near + 2))
    if near:
        for kind in (KW, KT2, KC1):
            gone(kind, blocks(2 * near))
        gone(KS1, blocks(2 * n_x - 2))
    if x_far:
        for kind in (KW2, KC3, KT3, KT4):
            gone(kind, blocks(2))
    gone(KP, p_send.at[pl.ds(0, n_z - 1)])
    gone(KX1, x1.at[pl.ds(0, n_z - 1)])
    gone(KX2, x2.at[pl.ds(0, n_z - 1)])
    gone(KB1, xb1.at[pl.ds(0, n_t - 1)])
    gone(KB2, xb2.at[pl.ds(0, n_t - 1)])
    for p in range(2):
        gone(KR + p, c_send.at[p])
        gone(KZ + p, z_send.at[p, pl.ds(0, n_z - 1)])
        if n_y > 1:
            gone(KY + p, y_recv.at[p, pl.ds(0, n_y - 1)])
        gone(KF + p, fin.at[p, 0, pl.ds(0, n_z - 1)])
        gone(KG + p, fin.at[p, 0])
    for store in stores:
        store.wait()


def shards(n_d, n_z, n_t, tokens, cotangent, w_query, w_key, w_value, w_out, masks, rig_ids):
    rows, width = tokens.shape[2], tokens.shape[3]
    depth = w_query.shape[1]
    lanes = 2 * depth
    smem = pl.BlockSpec(memory_space=pltpu.SMEM)
    hbm = pl.BlockSpec(memory_space=pltpu.HBM)
    half_block = (n_z, rows, lanes)
    _, places = receive_places(n_d, n_z, n_t)
    attended, grad_rows, grads = pl.pallas_call(
        functools.partial(kernel, n_d, n_z, n_t, depth),
        out_shape=(
            jax.ShapeDtypeStruct((rows, width), BF16),
            jax.ShapeDtypeStruct((rows, width), BF16),
            jax.ShapeDtypeStruct((2 * lanes, width), BF16),
        ),
        in_specs=[hbm] * 6 + [smem] * 2,
        out_specs=(hbm, hbm, hbm),
        scratch_shapes=[
            pltpu.VMEM((n_t, 2 * lanes, width), BF16),
            pltpu.VMEM((n_t, rows, width), BF16),
            pltpu.VMEM((n_t, rows, width), BF16),
            pltpu.VMEM((n_z, rows, 2 * lanes), BF16),
            pltpu.VMEM((n_z, rows, 2 * lanes), BF16),
            pltpu.VMEM((lanes, n_z * rows), BF16),
            pltpu.VMEM((n_z, n_z * rows, 2 * rows), BF16),
            pltpu.VMEM(half_block, BF16),
            pltpu.VMEM(half_block, BF16),
            pltpu.VMEM(half_block, BF16),
            pltpu.VMEM(half_block, BF16),
            pltpu.VMEM((n_t, rows, lanes), BF16),
            pltpu.VMEM((n_t, rows, lanes), BF16),
            pltpu.VMEM((2, lanes, width), F32),
            pltpu.VMEM((2, depth, width), BF16),
            pltpu.VMEM((2, depth, width), BF16),
            pltpu.VMEM((2, n_z, depth, width // n_z), BF16),
            pltpu.VMEM((2, n_z, depth, width // n_z), BF16),
            pltpu.VMEM((2, n_d // 2, depth, width // n_z), BF16),
            pltpu.VMEM((2, 2, n_z, depth, width // n_z), BF16),
            pltpu.VMEM((2 * rows, width), BF16),
            pltpu.VMEM((2 * lanes, width), BF16),
            pltpu.SemaphoreType.DMA((10,)),
            pltpu.SemaphoreType.DMA((KINDS,)),
            pltpu.SemaphoreType.DMA((places,)),
        ],
        compiler_params=pltpu.CompilerParams(
            collective_id=0, has_side_effects=True, vmem_limit_bytes=60 * 1024 * 1024
        ),
        cost_estimate=pl.CostEstimate(
            flops=3_000_000_000, bytes_accessed=8_000_000, transcendentals=1_000_000
        ),
    )(tokens.reshape(rows, width), cotangent.reshape(rows, width), w_query.T, w_key.T, w_value.T, w_out,
      masks, rig_ids)
    grads = grads.astype(F32)
    return (
        attended.reshape(tokens.shape),
        grad_rows.reshape(tokens.shape),
        grads[:depth].T,
        grads[lanes:lanes + depth].T,
        grads[lanes + depth:].T,
        grads[depth:lanes],
    )


def solution(mesh):
    sizes = mesh.shape
    return jax.shard_map(
        functools.partial(shards, sizes["dp"], sizes["view"], sizes["tm"]),
        mesh=mesh,
        in_specs=(
            P("dp", "view", "tm", None),
            P("dp", "view", "tm", None),
            P(None, "tm"),
            P(None, "tm"),
            P(None, "tm"),
            P("tm", None),
            P(),
            P("dp"),
        ),
        out_specs=(
            P("dp", "view", "tm", None),
            P("dp", "view", "tm", None),
            P(None, "tm"),
            P(None, "tm"),
            P(None, "tm"),
            P("tm", None),
        ),
        check_vma=False,
    )
```

```python
import functools

import jax
import jax.numpy as jnp
from jax import lax
from jax.experimental import pallas as pl
from jax.experimental.pallas import tpu as pltpu
from jax.sharding import PartitionSpec as P

MESH = pl.DeviceIdType.MESH
BF16 = jnp.bfloat16
F32 = jnp.float32

(KW, KV1, KV2, KS1, KS2, KT1, KT2, KC1, KC2, KP, KX1, KX2, KB1, KB2, KR, KZ, KY, KF, KG,
 KW2, KC3, KT3, KT4) = (*range(14), 14, 16, 18, 20, 22, *range(24, 28))
KINDS = 28

NT = (((1,), (1,)), ((), ()))


def dot(a, b):
    return jnp.dot(a, b, preferred_element_type=F32)


def dot_nt(a, b):
    return lax.dot_general(a, b, NT, preferred_element_type=F32)


def receive_places(n_d, n_z, n_t):
    n_x = n_t // 2
    sizes = [2 * n_x] + [n_x] * 8 + [1, n_z, n_z, 1, 1] + [1] * 6 + [n_z] * 2 + [1] * 2 + [2] * 4
    starts = [(sum(sizes[:k]), sizes[k]) for k in range(KINDS)]
    return starts, sum(sizes)


def kernel(
    n_d, n_z, n_t, depth,
    tok_hbm, cot_hbm, wq_hbm, wk_hbm, wv_hbm, wo_hbm, masks_ref, rig_ref,
    att_hbm, gtok_hbm, g_hbm,
    w_all, tok_all, cot_all, p_send, p_all, kv_t, pairs, x1, x2, xa1, xa2, xb1, xb2,
    g_sum, c_send, c_recv, z_send, z_recv, y_recv, fin, both_out, g_out,
    lsem, ssem, rsem,
):
    rows, width = tok_hbm.shape
    lanes = 2 * depth
    n_x = n_t // 2
    n_y = n_d // 2
    dp, z, tm = lax.axis_index("dp"), lax.axis_index("view"), lax.axis_index("tm")
    core, yh = dp % 2, dp // 2
    x, yl = tm // 2, tm % 2
    sib = dp + 1 - 2 * core
    pair = x * 2 + 1 - yl
    beyond = ((yh - 1 + 2 * yl + n_y) % n_y) * 2 + core

    loads = [
        pltpu.make_async_copy(src, dst, lsem.at[at])
        for at, (src, dst) in enumerate([
            (wq_hbm, w_all.at[tm, pl.ds(0, depth)]), (wo_hbm, w_all.at[tm, pl.ds(depth, depth)]),
            (wk_hbm, w_all.at[tm, pl.ds(lanes, depth)]),
            (wv_hbm, w_all.at[tm, pl.ds(lanes + depth, depth)]),
            (tok_hbm, tok_all.at[tm]), (cot_hbm, cot_all.at[tm]),
        ])
    ]
    for load in loads:
        load.start()

    starts, _ = receive_places(n_d, n_z, n_t)

    def copy(src, dst, kind, at, **to):
        start, size = starts[kind]
        place = start + at if size > 1 else start
        return pltpu.make_async_remote_copy(
            src_ref=src, dst_ref=dst, send_sem=ssem.at[kind], recv_sem=rsem.at[place],
            device_id=to, device_id_type=MESH,
        )

    def arrived(kind, ref):
        copy(ref, ref, kind, 0, dp=sib).wait_recv()

    def gone(kind, ref):
        copy(ref, ref, kind, 0, dp=sib).wait_send()

    def blocks(halves):
        if halves % 2:
            return tok_all.at[0, pl.ds(0, rows // 2)]
        return tok_all.at[pl.ds(0, halves // 2)]

    barrier = pltpu.get_barrier_semaphore()
    friends = [{"tm": (tm + s) % n_t} for s in range(1, n_t)]
    friends += [{"view": (z + s) % n_z} for s in range(1, n_z)]
    friends += [{"dp": (dp + 2 * s) % n_d} for s in range(1, n_y)]
    friends += [{"dp": sib}, {"dp": beyond, "tm": pair}]
    for friend in friends:
        pl.semaphore_signal(barrier, inc=1, device_id=friend, device_id_type=MESH)
    for load in loads:
        load.wait()
    pl.semaphore_wait(barrier, len(friends))

    def ahead(dx, side):
        return ((x + dx) % n_x) * 2 + side

    def behind(dx, side):
        return ((x - dx + n_x) % n_x) * 2 + side

    half, quarter = lanes, depth

    def w_rows(head, start, size):
        return w_all.at[head, pl.ds(pl.multiple_of(start, size), size)]

    def w_mine(head):
        return w_rows(head, core * half, half)

    def pieces(dx):
        return (1, 0) if dx == 1 else (0, 1)

    def w_along(dx, part):
        piece = w_rows(tm, core * half + part * quarter, quarter)
        return copy(piece, piece, KW, 2 * dx + part, tm=ahead(dx, yl))

    def w_across(dx, part):
        piece = w_rows(behind(dx, yl), core * half + part * quarter, quarter)
        if part == 0:
            return copy(piece, piece, KV1, dx, tm=pair)
        return copy(piece, piece, KV2, dx, dp=beyond, tm=pair)

    def w_share(dx, side, kind):
        part = w_mine(behind(dx, side))
        return copy(part, part, kind, dx, dp=sib)

    def w_shared(dx, side, kind):
        part = w_rows(behind(dx, side), (1 - core) * half, half)
        return copy(part, part, kind, dx, dp=sib)

    relays = [(1, 1), (3, 0)]

    def relay(ref, kind, side):
        if not x_far:
            return
        for dx, part in relays:
            rows_part = ref.at[behind(dx, side), pl.ds(part * (rows // 2), rows // 2)]
            copy(rows_part, rows_part, kind, part, tm=ahead(dx, yl)).start()

    def relayed(ref, kind, side):
        for dx in x_far:
            for part in range(2):
                rows_part = ref.at[behind(dx, side), pl.ds(part * (rows // 2), rows // 2)]
                copy(rows_part, rows_part, kind, part, tm=pair).wait_recv()

    def w_piece(dx, part):
        return w_rows(behind(dx, yl), core * half + part * quarter, quarter)

    x_near = [1, 3] if n_x == 4 else list(range(1, n_x))
    x_far = [2] if n_x == 4 else []
    x_order = x_near + x_far
    for turn in range(2):
        for dx in x_near:
            w_along(dx, pieces(dx)[turn]).start()
    for part in range(2):
        w_across(0, part).start()

    def tok_pair():
        return copy(tok_all.at[tm], tok_all.at[tm], KT1, 0, tm=pair)

    def tok_along(dx, span, kind):
        return copy(tok_all.at[span], tok_all.at[span], kind, dx, tm=ahead(dx, yl))

    def cot_pair(dx):
        span = behind(dx, yl)
        return copy(cot_all.at[span], cot_all.at[span], KC2, dx, tm=pair)

    def cot_along(dx):
        return copy(cot_all.at[tm], cot_all.at[tm], KC1, dx, tm=ahead(dx, yl))

    first = lax.broadcasted_iota(jnp.int32, (rows, lanes), 1) < depth

    def project(head):
        both = dot_nt(jnp.concatenate([tok_all[tm], cot_all[tm]], axis=0), w_all[head])
        p_send[head, :, :lanes] = jnp.where(first, both[:rows, :lanes], both[rows:, :lanes]).astype(BF16)
        p_send[head, :, lanes:] = both[:rows, lanes:].astype(BF16)

        @pl.when(head == z)
        def _():
            p_all[z] = p_send[head]

        @pl.when(head != z)
        def _():
            copy(p_send.at[head], p_all.at[z], KP, (head - z + n_z) % n_z, view=head).start()

    def w_arrive(dx, part):
        piece = w_piece(dx, part)
        if dx in x_far:
            copy(piece, piece, KW2, part, tm=pair).wait_recv()
        else:
            copy(piece, piece, KW, 2 * dx + part, tm=pair).wait_recv()
            if x_far and part == pieces(dx)[0]:
                copy(piece, piece, KW2, part, tm=ahead(dx, yl)).start()
        w_across(dx, part).start()

    def w_arrive_across(dx):
        head = behind(dx, 1 - yl)
        near = w_rows(head, core * half, quarter)
        far = w_rows(head, core * half + quarter, quarter)
        copy(near, near, KV1, dx, tm=pair).wait_recv()
        copy(far, far, KV2, dx, dp=beyond, tm=pair).wait_recv()
        w_share(dx, 1 - yl, KS2).start()

    def project_side(dxs, side, kind):
        def one(i, _):
            dx = dxs[0] + 2 * ((i + z) % len(dxs))
            w_shared(dx, side, kind).wait_recv()
            project(behind(dx, side))
            return 0

        if dxs:
            lax.fori_loop(0, len(dxs), one, 0)

    tok_pair().start()
    project(tm)
    w_arrive_across(0)
    for turn in range(2):
        for dx in x_near:
            w_arrive(dx, pieces(dx)[turn])
    for dx in x_near:
        w_share(dx, yl, KS1).start()
    project_side([0], 1 - yl, KS2)
    project_side(x_near, yl, KS1)
    for dx in x_far:
        for part in range(2):
            w_arrive(dx, part)
        w_share(dx, yl, KS1).start()
    for dx in x_near:
        w_arrive_across(dx)
    for dx in x_near:
        cot_along(dx).start()
        tok_along(dx, tm, KT1).start()
    project_side(x_near, 1 - yl, KS2)
    project_side(x_far, yl, KS1)
    for dx in x_far:
        w_arrive_across(dx)
    cot_pair(0).start()
    project_side(x_far, 1 - yl, KS2)

    for dx in x_near:
        span = behind(dx, yl)
        copy(cot_all.at[span], cot_all.at[span], KC1, dx, tm=pair).wait_recv()
        cot_pair(dx).start()
    relay(cot_all, KC3, yl)
    for dx in x_near:
        span = behind(dx, yl)
        copy(tok_all.at[span], tok_all.at[span], KT1, dx, tm=pair).wait_recv()
    relay(tok_all, KT3, yl)
    copy(tok_all.at[pair], tok_all.at[pair], KT1, 0, tm=pair).wait_recv()
    for dx in x_near:
        tok_along(dx, pair, KT2).start()

    arrived(KP, p_send.at[pl.ds(0, n_z - 1)])

    total = n_z * rows
    kv_t[...] = p_all[:, :, lanes:].reshape(total, lanes).T
    rig = rig_ref[0]
    factor = depth ** -0.5

    def split(cam):
        qd = p_all[cam, :, :lanes]
        zero = jnp.zeros_like(qd)
        return jnp.where(first, qd, zero), jnp.where(first, zero, qd)

    def attend(step, _):
        cams = [(z + 1 + 2 * step) % n_z, (z + 2 + 2 * step) % n_z]

        @pl.when(step == 0)
        def _():
            relayed(cot_all, KC3, yl)
            for dx in x_far:
                cot_pair(dx).start()

        @pl.when(step == 1)
        def _():
            for dx in x_near:
                span = behind(dx, 1 - yl)
                copy(tok_all.at[span], tok_all.at[span], KT2, dx, tm=pair).wait_recv()
            relay(tok_all, KT4, 1 - yl)

        query0, grad0 = split(cams[0])
        query1, grad1 = split(cams[1])
        kv = p_all[:, :, lanes:].reshape(total, lanes)
        both = dot_nt(kv, jnp.concatenate([query0, query1, grad0, grad1], axis=0))
        scores = jnp.concatenate(
            [
                jnp.concatenate(
                    [
                        both[b * rows:(b + 1) * rows, q * rows:(q + 1) * rows] * factor
                        + (masks_ref[rig, cams[q], b] - 1).astype(F32) * 1e30
                        for q in range(2)
                    ],
                    axis=1,
                )
                for b in range(n_z)
            ],
            axis=0,
        )
        weights = jnp.exp(scores - jnp.max(scores, axis=0, keepdims=True))
        probs = weights * (1.0 / jnp.sum(weights, axis=0, keepdims=True))
        probs_half = probs.astype(BF16)
        attn = dot(kv_t[depth:], probs_half)
        grad_attn = jnp.concatenate(
            [(query0 + grad0).astype(F32).T[depth:], (query1 + grad1).astype(F32).T[depth:]], axis=1
        )
        delta = jnp.sum(grad_attn * attn.astype(BF16).astype(F32), axis=0, keepdims=True)
        dscore = (probs * (both[:, 2 * rows:] - delta) * factor).astype(BF16)
        dq = dot(kv_t[:depth], dscore)
        out = jnp.concatenate([dq, attn], axis=0)
        for q, cam in enumerate(cams):
            cols = slice(q * rows, (q + 1) * rows)
            x1[cam] = out[:, cols].T.astype(BF16)

            @pl.when(cam == z)
            def _():
                xa1[z] = x1[cam]

            @pl.when(cam != z)
            def _():
                copy(x1.at[cam], xa1.at[z], KX1, (cam - z + n_z) % n_z, view=cam).start()

            pairs[cam, :, :rows] = dscore[:, cols]
            pairs[cam, :, rows:] = probs_half[:, cols]
        return 0

    lax.fori_loop(0, n_z // 2, attend, 0)

    def keys(step, _):
        cams = [(z + 1 + 2 * step) % n_z, (z + 2 + 2 * step) % n_z]
        sums = jnp.zeros((2 * rows, lanes), F32)
        for query in range(n_z):
            block = jnp.concatenate(split(query), axis=0)
            left = jnp.concatenate(
                [pairs[query, pl.ds(pl.multiple_of(cam * rows, rows), rows)] for cam in cams], axis=0
            )
            sums = sums + dot(left, block).astype(BF16).astype(F32)
        for k, cam in enumerate(cams):
            x2[cam] = sums[k * rows:(k + 1) * rows].astype(BF16)

            @pl.when(cam == z)
            def _():
                xa2[z] = x2[cam]

            @pl.when(cam != z)
            def _():
                copy(x2.at[cam], xa2.at[z], KX2, (cam - z + n_z) % n_z, view=cam).start()
        return 0

    lax.fori_loop(0, n_z // 2, keys, 0)

    def hand_on(src, dst, kind, head):
        @pl.when(head == tm)
        def _():
            dst[tm] = src[head]

        @pl.when(head != tm)
        def _():
            copy(src.at[head], dst.at[tm], kind, (head - tm + n_t) % n_t, tm=head).start()

    def arrive1(d, _):
        head = (z - d + n_z) % n_z

        @pl.when(d > 0)
        def _():
            copy(xa1.at[head], xa1.at[head], KX1, d, view=head).wait_recv()

        hand_on(xa1, xb1, KB1, head)
        return 0

    def arrive2(d, _):
        head = (z - d + n_z) % n_z

        @pl.when(d > 0)
        def _():
            copy(xa2.at[head], xa2.at[head], KX2, d, view=head).wait_recv()

        hand_on(xa2, xb2, KB2, head)
        return 0

    lax.fori_loop(0, n_z, lambda i, _: arrive1((i + tm) % n_z, _), 0)
    lax.fori_loop(0, n_z, lambda i, _: arrive2((i + tm) % n_z, _), 0)

    chunk = width // n_z
    keep = pl.multiple_of(core * depth, depth)
    give = pl.multiple_of((1 - core) * depth, depth)

    def core_copy(p):
        return copy(c_send.at[p], c_recv.at[p], KR + p, 0, dp=sib)

    def camera_copy(p, d):
        cam = (z + d) % n_z
        return copy(z_send.at[p, cam], z_recv.at[p, z], KZ + p, d, view=cam)

    def clip_copy(p, s):
        part = y_recv.at[p, yh]
        return copy(part, part, KY + p, s, dp=(dp + 2 * s) % n_d)

    def final_copy(p, d):
        part = fin.at[p, core, z]
        return copy(part, part, KF + p, d, view=(z + d) % n_z)

    def final_share(p, d):
        part = fin.at[p, core, (z - d + n_z) % n_z]
        return copy(part, part, KG + p, d, dp=sib)

    def core_start(p):
        c_send[p] = g_sum[p, pl.ds(give, depth)].astype(BF16)
        core_copy(p).start()

    def camera_start(p):
        core_copy(p).wait_recv()
        total = (g_sum[p, pl.ds(keep, depth)] + c_recv[p].astype(F32)).astype(BF16)
        for cam in range(n_z):
            z_send[p, cam] = total[:, cam * chunk:(cam + 1) * chunk]
        for d in range(1, n_z):
            camera_copy(p, d).start()

    def clip_start(p):
        total = z_send[p, z].astype(F32)
        arrived(KZ + p, z_recv.at[p, pl.ds(0, n_z - 1)])
        for d in range(1, n_z):
            total = total + z_recv[p, (z - d + n_z) % n_z].astype(F32)
        y_recv[p, yh] = total.astype(BF16)
        for s in range(1, n_y):
            clip_copy(p, s).start()

    def spread_start(p):
        if n_y > 1:
            arrived(KY + p, y_recv.at[p, pl.ds(0, n_y - 1)])
        total = y_recv[p, 0].astype(F32)
        for s in range(1, n_y):
            total = total + y_recv[p, s].astype(F32)
        fin[p, core, z] = total.astype(BF16)
        for d in range(1, n_z):
            final_copy(p, d).start()
        final_share(p, 0).start()

    def spread_forward(p):
        for d in range(1, n_z):
            part = fin.at[p, core, (z - d + n_z) % n_z]
            copy(part, part, KF + p, d, view=(z + d) % n_z).wait_recv()
            final_share(p, d).start()

    def spread_end(p):
        arrived(KG + p, fin.at[p, 1 - core])
        for side in range(2):
            for cam in range(n_z):
                place = (slice((2 * p + side) * depth, (2 * p + side + 1) * depth),
                         slice(cam * chunk, (cam + 1) * chunk))
                g_out[place] = fin[p, side, cam].astype(F32)
        return g_store(p)

    def g_store(p):
        part = pl.ds(p * lanes, lanes)
        return pltpu.make_async_copy(g_out.at[part], g_hbm.at[part], lsem.at[8 + p])

    def finish(head, sums):
        one, two = xa1[head], xa2[head]
        zero = jnp.zeros_like(one)
        left = jnp.concatenate(
            [
                jnp.concatenate([jnp.where(first, one, zero), two], axis=1),
                jnp.concatenate([jnp.where(first, zero, one), zero], axis=1),
            ],
            axis=0,
        )
        return sums + dot(left, w_all[head])

    relayed(tok_all, KT3, yl)
    relayed(tok_all, KT4, 1 - yl)
    for dx in [0] + x_order:
        other = behind(dx, 1 - yl)
        copy(cot_all.at[other], cot_all.at[other], KC2, dx, tm=pair).wait_recv()
    tokens = tok_all[...].reshape(n_t * rows, width)
    cots = cot_all[...].reshape(n_t * rows, width)
    arrived(KB1, xb1.at[pl.ds(0, n_t - 1)])
    b1 = xb1[...].reshape(n_t * rows, lanes).T
    g_sum[0, :depth] = dot(b1[:depth], tokens)
    g_sum[0, depth:] = dot(b1[depth:], cots)
    core_start(0)
    arrived(KB2, xb2.at[pl.ds(0, n_t - 1)])
    g_sum[1] = dot(xb2[...].reshape(n_t * rows, lanes).T, tokens)
    camera_start(0)
    core_start(1)
    camera_start(1)
    sums = lax.fori_loop(0, n_z // 2, finish, jnp.zeros((2 * rows, width), F32))
    clip_start(0)
    sums = lax.fori_loop(n_z // 2, n_z, finish, sums)
    both_out[...] = sums.astype(BF16)
    stores = [
        pltpu.make_async_copy(both_out.at[pl.ds(0, rows)], gtok_hbm, lsem.at[6]),
        pltpu.make_async_copy(both_out.at[pl.ds(rows, rows)], att_hbm, lsem.at[7]),
    ]
    for store in stores:
        store.start()
    clip_start(1)
    spread_start(0)
    spread_start(1)
    spread_forward(0)
    stores.append(spread_end(0))
    stores[-1].start()
    spread_forward(1)
    stores.append(spread_end(1))
    stores[-1].start()

    near = len(x_near)
    gone(KV1, blocks(n_x))
    gone(KV2, blocks(n_x))
    gone(KS2, blocks(2 * n_x))
    gone(KC2, blocks(2 * n_x))
    gone(KT1, blocks(2 * near + 2))
    if near:
        for kind in (KW, KT2, KC1):
            gone(kind, blocks(2 * near))
        gone(KS1, blocks(2 * n_x - 2))
    if x_far:
        for kind in (KW2, KC3, KT3, KT4):
            gone(kind, blocks(2))
    gone(KP, p_send.at[pl.ds(0, n_z - 1)])
    gone(KX1, x1.at[pl.ds(0, n_z - 1)])
    gone(KX2, x2.at[pl.ds(0, n_z - 1)])
    gone(KB1, xb1.at[pl.ds(0, n_t - 1)])
    gone(KB2, xb2.at[pl.ds(0, n_t - 1)])
    for p in range(2):
        gone(KR + p, c_send.at[p])
        gone(KZ + p, z_send.at[p, pl.ds(0, n_z - 1)])
        if n_y > 1:
            gone(KY + p, y_recv.at[p, pl.ds(0, n_y - 1)])
        gone(KF + p, fin.at[p, 0, pl.ds(0, n_z - 1)])
        gone(KG + p, fin.at[p, 0])
    for store in stores:
        store.wait()


def shards(n_d, n_z, n_t, tokens, cotangent, w_query, w_key, w_value, w_out, masks, rig_ids):
    rows, width = tokens.shape[2], tokens.shape[3]
    depth = w_query.shape[1]
    lanes = 2 * depth
    smem = pl.BlockSpec(memory_space=pltpu.SMEM)
    hbm = pl.BlockSpec(memory_space=pltpu.HBM)
    half_block = (n_z, rows, lanes)
    _, places = receive_places(n_d, n_z, n_t)
    attended, grad_rows, grads = pl.pallas_call(
        functools.partial(kernel, n_d, n_z, n_t, depth),
        out_shape=(
            jax.ShapeDtypeStruct((rows, width), BF16),
            jax.ShapeDtypeStruct((rows, width), BF16),
            jax.ShapeDtypeStruct((2 * lanes, width), F32),
        ),
        in_specs=[hbm] * 6 + [smem] * 2,
        out_specs=(hbm, hbm, hbm),
        scratch_shapes=[
            pltpu.VMEM((n_t, 2 * lanes, width), BF16),
            pltpu.VMEM((n_t, rows, width), BF16),
            pltpu.VMEM((n_t, rows, width), BF16),
            pltpu.VMEM((n_z, rows, 2 * lanes), BF16),
            pltpu.VMEM((n_z, rows, 2 * lanes), BF16),
            pltpu.VMEM((lanes, n_z * rows), BF16),
            pltpu.VMEM((n_z, n_z * rows, 2 * rows), BF16),
            pltpu.VMEM(half_block, BF16),
            pltpu.VMEM(half_block, BF16),
            pltpu.VMEM(half_block, BF16),
            pltpu.VMEM(half_block, BF16),
            pltpu.VMEM((n_t, rows, lanes), BF16),
            pltpu.VMEM((n_t, rows, lanes), BF16),
            pltpu.VMEM((2, lanes, width), F32),
            pltpu.VMEM((2, depth, width), BF16),
            pltpu.VMEM((2, depth, width), BF16),
            pltpu.VMEM((2, n_z, depth, width // n_z), BF16),
            pltpu.VMEM((2, n_z, depth, width // n_z), BF16),
            pltpu.VMEM((2, n_d // 2, depth, width // n_z), BF16),
            pltpu.VMEM((2, 2, n_z, depth, width // n_z), BF16),
            pltpu.VMEM((2 * rows, width), BF16),
            pltpu.VMEM((2 * lanes, width), F32),
            pltpu.SemaphoreType.DMA((10,)),
            pltpu.SemaphoreType.DMA((KINDS,)),
            pltpu.SemaphoreType.DMA((places,)),
        ],
        compiler_params=pltpu.CompilerParams(
            collective_id=0, has_side_effects=True, vmem_limit_bytes=60 * 1024 * 1024
        ),
        cost_estimate=pl.CostEstimate(
            flops=3_000_000_000, bytes_accessed=8_000_000, transcendentals=1_000_000
        ),
    )(tokens.reshape(rows, width), cotangent.reshape(rows, width), w_query.T, w_key.T, w_value.T, w_out,
      masks, rig_ids)
    return (
        attended.reshape(tokens.shape),
        grad_rows.reshape(tokens.shape),
        grads[:depth].T,
        grads[lanes:lanes + depth].T,
        grads[lanes + depth:].T,
        grads[depth:lanes],
    )


def solution(mesh):
    sizes = mesh.shape
    return jax.shard_map(
        functools.partial(shards, sizes["dp"], sizes["view"], sizes["tm"]),
        mesh=mesh,
        in_specs=(
            P("dp", "view", "tm", None),
            P("dp", "view", "tm", None),
            P(None, "tm"),
            P(None, "tm"),
            P(None, "tm"),
            P("tm", None),
            P(),
            P("dp"),
        ),
        out_specs=(
            P("dp", "view", "tm", None),
            P("dp", "view", "tm", None),
            P(None, "tm"),
            P(None, "tm"),
            P(None, "tm"),
            P("tm", None),
        ),
        check_vma=False,
    )
```

```python
import functools

import jax
import jax.numpy as jnp
from jax import lax
from jax.experimental import pallas as pl
from jax.experimental.pallas import tpu as pltpu
from jax.sharding import PartitionSpec as P

MESH = pl.DeviceIdType.MESH
BF16 = jnp.bfloat16
F32 = jnp.float32

(KW, KV1, KV2, KS1, KS2, KT1, KT2, KC1, KC2, KP, KX1, KX2, KB1, KB2, KR, KZ, KY, KF, KG,
 KW2, KC3, KT3, KT4) = (*range(14), 14, 16, 18, 20, 22, *range(24, 28))
KINDS = 28

NT = (((1,), (1,)), ((), ()))


def dot(a, b):
    return jnp.dot(a, b, preferred_element_type=F32)


def dot_nt(a, b):
    return lax.dot_general(a, b, NT, preferred_element_type=F32)


def receive_places(n_d, n_z, n_t):
    n_x = n_t // 2
    sizes = [2 * n_x] + [n_x] * 8 + [1, n_z, n_z, 1, 1] + [1] * 6 + [n_z] * 2 + [1] * 2 + [2] * 4
    starts = [(sum(sizes[:k]), sizes[k]) for k in range(KINDS)]
    return starts, sum(sizes)


def kernel(
    n_d, n_z, n_t, depth,
    tok_hbm, cot_hbm, wq_hbm, wk_hbm, wv_hbm, wo_hbm, masks_ref, rig_ref,
    att_hbm, gtok_hbm, g_hbm,
    w_all, tok_all, cot_all, p_send, p_all, kv_t, pairs, x1, x2, xa1, xa2, xb1, xb2,
    g_sum, c_send, c_recv, z_send, z_recv, y_recv, fin, both_out, g_out,
    lsem, ssem, rsem,
):
    rows, width = tok_hbm.shape
    lanes = 2 * depth
    n_x = n_t // 2
    n_y = n_d // 2
    dp, z, tm = lax.axis_index("dp"), lax.axis_index("view"), lax.axis_index("tm")
    core, yh = dp % 2, dp // 2
    x, yl = tm // 2, tm % 2
    sib = dp + 1 - 2 * core
    pair = x * 2 + 1 - yl
    beyond = ((yh - 1 + 2 * yl + n_y) % n_y) * 2 + core

    loads = [
        pltpu.make_async_copy(src, dst, lsem.at[at])
        for at, (src, dst) in enumerate([
            (wq_hbm, w_all.at[tm, pl.ds(0, depth)]), (wo_hbm, w_all.at[tm, pl.ds(depth, depth)]),
            (wk_hbm, w_all.at[tm, pl.ds(lanes, depth)]),
            (wv_hbm, w_all.at[tm, pl.ds(lanes + depth, depth)]),
            (tok_hbm, tok_all.at[tm]), (cot_hbm, cot_all.at[tm]),
        ])
    ]
    for load in loads:
        load.start()

    starts, _ = receive_places(n_d, n_z, n_t)

    def copy(src, dst, kind, at, **to):
        start, size = starts[kind]
        place = start + at if size > 1 else start
        return pltpu.make_async_remote_copy(
            src_ref=src, dst_ref=dst, send_sem=ssem.at[kind], recv_sem=rsem.at[place],
            device_id=to, device_id_type=MESH,
        )

    def arrived(kind, ref):
        copy(ref, ref, kind, 0, dp=sib).wait_recv()

    def gone(kind, ref):
        copy(ref, ref, kind, 0, dp=sib).wait_send()

    def blocks(halves):
        if halves % 2:
            return tok_all.at[0, pl.ds(0, rows // 2)]
        return tok_all.at[pl.ds(0, halves // 2)]

    barrier = pltpu.get_barrier_semaphore()
    friends = [{"tm": (tm + s) % n_t} for s in range(1, n_t)]
    friends += [{"view": (z + s) % n_z} for s in range(1, n_z)]
    friends += [{"dp": (dp + 2 * s) % n_d} for s in range(1, n_y)]
    friends += [{"dp": sib}, {"dp": beyond, "tm": pair}]
    for friend in friends:
        pl.semaphore_signal(barrier, inc=1, device_id=friend, device_id_type=MESH)
    for load in loads:
        load.wait()
    pl.semaphore_wait(barrier, len(friends))

    def ahead(dx, side):
        return ((x + dx) % n_x) * 2 + side

    def behind(dx, side):
        return ((x - dx + n_x) % n_x) * 2 + side

    half, quarter = lanes, depth

    def w_rows(head, start, size):
        return w_all.at[head, pl.ds(pl.multiple_of(start, size), size)]

    def w_mine(head):
        return w_rows(head, core * half, half)

    def pieces(dx):
        return (1, 0) if dx == 1 else (0, 1)

    def w_along(dx, part):
        piece = w_rows(tm, core * half + part * quarter, quarter)
        return copy(piece, piece, KW, 2 * dx + part, tm=ahead(dx, yl))

    def w_across(dx, part):
        piece = w_rows(behind(dx, yl), core * half + part * quarter, quarter)
        if part == 0:
            return copy(piece, piece, KV1, dx, tm=pair)
        return copy(piece, piece, KV2, dx, dp=beyond, tm=pair)

    def w_share(dx, side, kind):
        part = w_mine(behind(dx, side))
        return copy(part, part, kind, dx, dp=sib)

    def w_shared(dx, side, kind):
        part = w_rows(behind(dx, side), (1 - core) * half, half)
        return copy(part, part, kind, dx, dp=sib)

    relays = [(1, 1), (3, 0)]

    def relay(ref, kind, side):
        if not x_far:
            return
        for dx, part in relays:
            rows_part = ref.at[behind(dx, side), pl.ds(part * (rows // 2), rows // 2)]
            copy(rows_part, rows_part, kind, part, tm=ahead(dx, yl)).start()

    def relayed(ref, kind, side):
        for dx in x_far:
            for part in range(2):
                rows_part = ref.at[behind(dx, side), pl.ds(part * (rows // 2), rows // 2)]
                copy(rows_part, rows_part, kind, part, tm=pair).wait_recv()

    def w_piece(dx, part):
        return w_rows(behind(dx, yl), core * half + part * quarter, quarter)

    x_near = [1, 3] if n_x == 4 else list(range(1, n_x))
    x_far = [2] if n_x == 4 else []
    x_order = x_near + x_far
    for turn in range(2):
        for dx in x_near:
            w_along(dx, pieces(dx)[turn]).start()
    for part in range(2):
        w_across(0, part).start()

    def tok_pair():
        return copy(tok_all.at[tm], tok_all.at[tm], KT1, 0, tm=pair)

    def tok_along(dx, span, kind):
        return copy(tok_all.at[span], tok_all.at[span], kind, dx, tm=ahead(dx, yl))

    def cot_pair(dx):
        span = behind(dx, yl)
        return copy(cot_all.at[span], cot_all.at[span], KC2, dx, tm=pair)

    def cot_along(dx):
        return copy(cot_all.at[tm], cot_all.at[tm], KC1, dx, tm=ahead(dx, yl))

    first = lax.broadcasted_iota(jnp.int32, (rows, lanes), 1) < depth

    def project(head):
        both = dot_nt(jnp.concatenate([tok_all[tm], cot_all[tm]], axis=0), w_all[head])
        p_send[head, :, :lanes] = jnp.where(first, both[:rows, :lanes], both[rows:, :lanes]).astype(BF16)
        p_send[head, :, lanes:] = both[:rows, lanes:].astype(BF16)

        @pl.when(head == z)
        def _():
            p_all[z] = p_send[head]

        @pl.when(head != z)
        def _():
            copy(p_send.at[head], p_all.at[z], KP, (head - z + n_z) % n_z, view=head).start()

    def w_arrive(dx, part):
        piece = w_piece(dx, part)
        if dx in x_far:
            copy(piece, piece, KW2, part, tm=pair).wait_recv()
        else:
            copy(piece, piece, KW, 2 * dx + part, tm=pair).wait_recv()
            if x_far and part == pieces(dx)[0]:
                copy(piece, piece, KW2, part, tm=ahead(dx, yl)).start()
        w_across(dx, part).start()

    def w_arrive_across(dx):
        head = behind(dx, 1 - yl)
        near = w_rows(head, core * half, quarter)
        far = w_rows(head, core * half + quarter, quarter)
        copy(near, near, KV1, dx, tm=pair).wait_recv()
        copy(far, far, KV2, dx, dp=beyond, tm=pair).wait_recv()
        w_share(dx, 1 - yl, KS2).start()

    def project_side(dxs, side, kind):
        def one(i, _):
            dx = dxs[0] + 2 * ((i + z) % len(dxs))
            w_shared(dx, side, kind).wait_recv()
            project(behind(dx, side))
            return 0

        if dxs:
            lax.fori_loop(0, len(dxs), one, 0)

    tok_pair().start()
    project(tm)
    w_arrive_across(0)
    for turn in range(2):
        for dx in x_near:
            w_arrive(dx, pieces(dx)[turn])
    for dx in x_near:
        w_share(dx, yl, KS1).start()
    project_side([0], 1 - yl, KS2)
    project_side(x_near, yl, KS1)
    for dx in x_near:
        cot_along(dx).start()
    for dx in x_far:
        for part in range(2):
            w_arrive(dx, part)
        w_share(dx, yl, KS1).start()
    for dx in x_near:
        w_arrive_across(dx)
    for dx in x_near:
        tok_along(dx, tm, KT1).start()
    project_side(x_near, 1 - yl, KS2)
    project_side(x_far, yl, KS1)
    for dx in x_far:
        w_arrive_across(dx)
    cot_pair(0).start()
    project_side(x_far, 1 - yl, KS2)

    for dx in x_near:
        span = behind(dx, yl)
        copy(cot_all.at[span], cot_all.at[span], KC1, dx, tm=pair).wait_recv()
        cot_pair(dx).start()
    relay(cot_all, KC3, yl)
    for dx in x_near:
        span = behind(dx, yl)
        copy(tok_all.at[span], tok_all.at[span], KT1, dx, tm=pair).wait_recv()
    relay(tok_all, KT3, yl)
    copy(tok_all.at[pair], tok_all.at[pair], KT1, 0, tm=pair).wait_recv()
    for dx in x_near:
        tok_along(dx, pair, KT2).start()

    arrived(KP, p_send.at[pl.ds(0, n_z - 1)])

    total = n_z * rows
    kv_t[...] = p_all[:, :, lanes:].reshape(total, lanes).T
    rig = rig_ref[0]
    factor = depth ** -0.5

    def split(cam):
        qd = p_all[cam, :, :lanes]
        zero = jnp.zeros_like(qd)
        return jnp.where(first, qd, zero), jnp.where(first, zero, qd)

    def attend(step, _):
        cams = [(z + 1 + 2 * step) % n_z, (z + 2 + 2 * step) % n_z]

        @pl.when(step == 0)
        def _():
            relayed(cot_all, KC3, yl)
            for dx in x_far:
                cot_pair(dx).start()

        @pl.when(step == 1)
        def _():
            for dx in x_near:
                span = behind(dx, 1 - yl)
                copy(tok_all.at[span], tok_all.at[span], KT2, dx, tm=pair).wait_recv()
            relay(tok_all, KT4, 1 - yl)

        query0, grad0 = split(cams[0])
        query1, grad1 = split(cams[1])
        kv = p_all[:, :, lanes:].reshape(total, lanes)
        both = dot_nt(kv, jnp.concatenate([query0, query1, grad0, grad1], axis=0))
        scores = jnp.concatenate(
            [
                jnp.concatenate(
                    [
                        both[b * rows:(b + 1) * rows, q * rows:(q + 1) * rows] * factor
                        + (masks_ref[rig, cams[q], b] - 1).astype(F32) * 1e30
                        for q in range(2)
                    ],
                    axis=1,
                )
                for b in range(n_z)
            ],
            axis=0,
        )
        weights = jnp.exp(scores - jnp.max(scores, axis=0, keepdims=True))
        probs = weights * (1.0 / jnp.sum(weights, axis=0, keepdims=True))
        probs_half = probs.astype(BF16)
        attn = dot(kv_t[depth:], probs_half)
        grad_attn = jnp.concatenate(
            [(query0 + grad0).astype(F32).T[depth:], (query1 + grad1).astype(F32).T[depth:]], axis=1
        )
        delta = jnp.sum(grad_attn * attn.astype(BF16).astype(F32), axis=0, keepdims=True)
        dscore = (probs * (both[:, 2 * rows:] - delta) * factor).astype(BF16)
        dq = dot(kv_t[:depth], dscore)
        out = jnp.concatenate([dq, attn], axis=0)
        for q, cam in enumerate(cams):
            cols = slice(q * rows, (q + 1) * rows)
            x1[cam] = out[:, cols].T.astype(BF16)

            @pl.when(cam == z)
            def _():
                xa1[z] = x1[cam]

            @pl.when(cam != z)
            def _():
                copy(x1.at[cam], xa1.at[z], KX1, (cam - z + n_z) % n_z, view=cam).start()

            pairs[cam, :, :rows] = dscore[:, cols]
            pairs[cam, :, rows:] = probs_half[:, cols]
        return 0

    lax.fori_loop(0, n_z // 2, attend, 0)

    def keys(step, _):
        cams = [(z + 1 + 2 * step) % n_z, (z + 2 + 2 * step) % n_z]
        sums = jnp.zeros((2 * rows, lanes), F32)
        for query in range(n_z):
            block = jnp.concatenate(split(query), axis=0)
            left = jnp.concatenate(
                [pairs[query, pl.ds(pl.multiple_of(cam * rows, rows), rows)] for cam in cams], axis=0
            )
            sums = sums + dot(left, block).astype(BF16).astype(F32)
        for k, cam in enumerate(cams):
            x2[cam] = sums[k * rows:(k + 1) * rows].astype(BF16)

            @pl.when(cam == z)
            def _():
                xa2[z] = x2[cam]

            @pl.when(cam != z)
            def _():
                copy(x2.at[cam], xa2.at[z], KX2, (cam - z + n_z) % n_z, view=cam).start()
        return 0

    lax.fori_loop(0, n_z // 2, keys, 0)

    def hand_on(src, dst, kind, head):
        @pl.when(head == tm)
        def _():
            dst[tm] = src[head]

        @pl.when(head != tm)
        def _():
            copy(src.at[head], dst.at[tm], kind, (head - tm + n_t) % n_t, tm=head).start()

    def arrive1(d, _):
        head = (z - d + n_z) % n_z

        @pl.when(d > 0)
        def _():
            copy(xa1.at[head], xa1.at[head], KX1, d, view=head).wait_recv()

        hand_on(xa1, xb1, KB1, head)
        return 0

    def arrive2(d, _):
        head = (z - d + n_z) % n_z

        @pl.when(d > 0)
        def _():
            copy(xa2.at[head], xa2.at[head], KX2, d, view=head).wait_recv()

        hand_on(xa2, xb2, KB2, head)
        return 0

    lax.fori_loop(0, n_z, lambda i, _: arrive1((i + tm) % n_z, _), 0)
    lax.fori_loop(0, n_z, lambda i, _: arrive2((i + tm) % n_z, _), 0)

    chunk = width // n_z
    keep = pl.multiple_of(core * depth, depth)
    give = pl.multiple_of((1 - core) * depth, depth)

    def core_copy(p):
        return copy(c_send.at[p], c_recv.at[p], KR + p, 0, dp=sib)

    def camera_copy(p, d):
        cam = (z + d) % n_z
        return copy(z_send.at[p, cam], z_recv.at[p, z], KZ + p, d, view=cam)

    def clip_copy(p, s):
        part = y_recv.at[p, yh]
        return copy(part, part, KY + p, s, dp=(dp + 2 * s) % n_d)

    def final_copy(p, d):
        part = fin.at[p, core, z]
        return copy(part, part, KF + p, d, view=(z + d) % n_z)

    def final_share(p, d):
        part = fin.at[p, core, (z - d + n_z) % n_z]
        return copy(part, part, KG + p, d, dp=sib)

    def core_start(p):
        c_send[p] = g_sum[p, pl.ds(give, depth)].astype(BF16)
        core_copy(p).start()

    def camera_start(p):
        core_copy(p).wait_recv()
        total = (g_sum[p, pl.ds(keep, depth)] + c_recv[p].astype(F32)).astype(BF16)
        for cam in range(n_z):
            z_send[p, cam] = total[:, cam * chunk:(cam + 1) * chunk]
        for d in range(1, n_z):
            camera_copy(p, d).start()

    def clip_start(p):
        total = z_send[p, z].astype(F32)
        arrived(KZ + p, z_recv.at[p, pl.ds(0, n_z - 1)])
        for d in range(1, n_z):
            total = total + z_recv[p, (z - d + n_z) % n_z].astype(F32)
        y_recv[p, yh] = total.astype(BF16)
        for s in range(1, n_y):
            clip_copy(p, s).start()

    def spread_start(p):
        if n_y > 1:
            arrived(KY + p, y_recv.at[p, pl.ds(0, n_y - 1)])
        total = y_recv[p, 0].astype(F32)
        for s in range(1, n_y):
            total = total + y_recv[p, s].astype(F32)
        fin[p, core, z] = total.astype(BF16)
        for d in range(1, n_z):
            final_copy(p, d).start()
        final_share(p, 0).start()

    def spread_forward(p):
        for d in range(1, n_z):
            part = fin.at[p, core, (z - d + n_z) % n_z]
            copy(part, part, KF + p, d, view=(z + d) % n_z).wait_recv()
            final_share(p, d).start()

    def spread_end(p):
        arrived(KG + p, fin.at[p, 1 - core])
        for side in range(2):
            for cam in range(n_z):
                place = (slice((2 * p + side) * depth, (2 * p + side + 1) * depth),
                         slice(cam * chunk, (cam + 1) * chunk))
                g_out[place] = fin[p, side, cam].astype(F32)
        return g_store(p)

    def g_store(p):
        part = pl.ds(p * lanes, lanes)
        return pltpu.make_async_copy(g_out.at[part], g_hbm.at[part], lsem.at[8 + p])

    def finish(head, sums):
        one, two = xa1[head], xa2[head]
        zero = jnp.zeros_like(one)
        left = jnp.concatenate(
            [
                jnp.concatenate([jnp.where(first, one, zero), two], axis=1),
                jnp.concatenate([jnp.where(first, zero, one), zero], axis=1),
            ],
            axis=0,
        )
        return sums + dot(left, w_all[head])

    relayed(tok_all, KT3, yl)
    relayed(tok_all, KT4, 1 - yl)
    for dx in [0] + x_order:
        other = behind(dx, 1 - yl)
        copy(cot_all.at[other], cot_all.at[other], KC2, dx, tm=pair).wait_recv()
    tokens = tok_all[...].reshape(n_t * rows, width)
    cots = cot_all[...].reshape(n_t * rows, width)
    arrived(KB1, xb1.at[pl.ds(0, n_t - 1)])
    b1 = xb1[...].reshape(n_t * rows, lanes).T
    g_sum[0, :depth] = dot(b1[:depth], tokens)
    g_sum[0, depth:] = dot(b1[depth:], cots)
    core_start(0)
    arrived(KB2, xb2.at[pl.ds(0, n_t - 1)])
    g_sum[1] = dot(xb2[...].reshape(n_t * rows, lanes).T, tokens)
    camera_start(0)
    core_start(1)
    camera_start(1)
    sums = lax.fori_loop(0, n_z // 2, finish, jnp.zeros((2 * rows, width), F32))
    clip_start(0)
    sums = lax.fori_loop(n_z // 2, n_z, finish, sums)
    both_out[...] = sums.astype(BF16)
    stores = [
        pltpu.make_async_copy(both_out.at[pl.ds(0, rows)], gtok_hbm, lsem.at[6]),
        pltpu.make_async_copy(both_out.at[pl.ds(rows, rows)], att_hbm, lsem.at[7]),
    ]
    for store in stores:
        store.start()
    clip_start(1)
    spread_start(0)
    spread_start(1)
    spread_forward(0)
    stores.append(spread_end(0))
    stores[-1].start()
    spread_forward(1)
    stores.append(spread_end(1))
    stores[-1].start()

    near = len(x_near)
    gone(KV1, blocks(n_x))
    gone(KV2, blocks(n_x))
    gone(KS2, blocks(2 * n_x))
    gone(KC2, blocks(2 * n_x))
    gone(KT1, blocks(2 * near + 2))
    if near:
        for kind in (KW, KT2, KC1):
            gone(kind, blocks(2 * near))
        gone(KS1, blocks(2 * n_x - 2))
    if x_far:
        for kind in (KW2, KC3, KT3, KT4):
            gone(kind, blocks(2))
    gone(KP, p_send.at[pl.ds(0, n_z - 1)])
    gone(KX1, x1.at[pl.ds(0, n_z - 1)])
    gone(KX2, x2.at[pl.ds(0, n_z - 1)])
    gone(KB1, xb1.at[pl.ds(0, n_t - 1)])
    gone(KB2, xb2.at[pl.ds(0, n_t - 1)])
    for p in range(2):
        gone(KR + p, c_send.at[p])
        gone(KZ + p, z_send.at[p, pl.ds(0, n_z - 1)])
        if n_y > 1:
            gone(KY + p, y_recv.at[p, pl.ds(0, n_y - 1)])
        gone(KF + p, fin.at[p, 0, pl.ds(0, n_z - 1)])
        gone(KG + p, fin.at[p, 0])
    for store in stores:
        store.wait()


def shards(n_d, n_z, n_t, tokens, cotangent, w_query, w_key, w_value, w_out, masks, rig_ids):
    rows, width = tokens.shape[2], tokens.shape[3]
    depth = w_query.shape[1]
    lanes = 2 * depth
    smem = pl.BlockSpec(memory_space=pltpu.SMEM)
    hbm = pl.BlockSpec(memory_space=pltpu.HBM)
    half_block = (n_z, rows, lanes)
    _, places = receive_places(n_d, n_z, n_t)
    attended, grad_rows, grads = pl.pallas_call(
        functools.partial(kernel, n_d, n_z, n_t, depth),
        out_shape=(
            jax.ShapeDtypeStruct((rows, width), BF16),
            jax.ShapeDtypeStruct((rows, width), BF16),
            jax.ShapeDtypeStruct((2 * lanes, width), F32),
        ),
        in_specs=[hbm] * 6 + [smem] * 2,
        out_specs=(hbm, hbm, hbm),
        scratch_shapes=[
            pltpu.VMEM((n_t, 2 * lanes, width), BF16),
            pltpu.VMEM((n_t, rows, width), BF16),
            pltpu.VMEM((n_t, rows, width), BF16),
            pltpu.VMEM((n_z, rows, 2 * lanes), BF16),
            pltpu.VMEM((n_z, rows, 2 * lanes), BF16),
            pltpu.VMEM((lanes, n_z * rows), BF16),
            pltpu.VMEM((n_z, n_z * rows, 2 * rows), BF16),
            pltpu.VMEM(half_block, BF16),
            pltpu.VMEM(half_block, BF16),
            pltpu.VMEM(half_block, BF16),
            pltpu.VMEM(half_block, BF16),
            pltpu.VMEM((n_t, rows, lanes), BF16),
            pltpu.VMEM((n_t, rows, lanes), BF16),
            pltpu.VMEM((2, lanes, width), F32),
            pltpu.VMEM((2, depth, width), BF16),
            pltpu.VMEM((2, depth, width), BF16),
            pltpu.VMEM((2, n_z, depth, width // n_z), BF16),
            pltpu.VMEM((2, n_z, depth, width // n_z), BF16),
            pltpu.VMEM((2, n_d // 2, depth, width // n_z), BF16),
            pltpu.VMEM((2, 2, n_z, depth, width // n_z), BF16),
            pltpu.VMEM((2 * rows, width), BF16),
            pltpu.VMEM((2 * lanes, width), F32),
            pltpu.SemaphoreType.DMA((10,)),
            pltpu.SemaphoreType.DMA((KINDS,)),
            pltpu.SemaphoreType.DMA((places,)),
        ],
        compiler_params=pltpu.CompilerParams(
            collective_id=0, has_side_effects=True, vmem_limit_bytes=60 * 1024 * 1024
        ),
        cost_estimate=pl.CostEstimate(
            flops=3_000_000_000, bytes_accessed=8_000_000, transcendentals=1_000_000
        ),
    )(tokens.reshape(rows, width), cotangent.reshape(rows, width), w_query.T, w_key.T, w_value.T, w_out,
      masks, rig_ids)
    return (
        attended.reshape(tokens.shape),
        grad_rows.reshape(tokens.shape),
        grads[:depth].T,
        grads[lanes:lanes + depth].T,
        grads[lanes + depth:].T,
        grads[depth:lanes],
    )


def solution(mesh):
    sizes = mesh.shape
    return jax.shard_map(
        functools.partial(shards, sizes["dp"], sizes["view"], sizes["tm"]),
        mesh=mesh,
        in_specs=(
            P("dp", "view", "tm", None),
            P("dp", "view", "tm", None),
            P(None, "tm"),
            P(None, "tm"),
            P(None, "tm"),
            P("tm", None),
            P(),
            P("dp"),
        ),
        out_specs=(
            P("dp", "view", "tm", None),
            P("dp", "view", "tm", None),
            P(None, "tm"),
            P(None, "tm"),
            P(None, "tm"),
            P("tm", None),
        ),
        check_vma=False,
    )
```
